256 devices in a mesh: lat: 64 (over y_lo, z, x), lon: 4 (over y_hi, core).
Axes of the slice: x: 4, y: 4 (y_hi: 2, y_lo: 2; y = y_hi * 2 + y_lo), z: 8, core: 2. Of those that a mesh axis runs over, the one named last changes fastest.
Arguments:
- grid_latent: bfloat16 [64, 4, 256, 512], P('lat', 'lon'), may hold values from -6 to 6
- mesh_latent: bfloat16 [256, 64, 512], P('lat', 'lon'), may hold values from -6 to 6
- cotangent: bfloat16 [64, 4, 256, 227], P('lat', 'lon'), may hold values from -6 to 6
- neighbours: int32 [64, 4, 3, 256], P('lat', 'lon'), may hold values from 0 to 106, as said below
- live: int32 [64, 4], P('lat', 'lon'), may hold values from 64 to 256, as said below
- w_em: bfloat16 [512, 512], replicated, may hold values from -0.25 to 0.25
- w_eg: bfloat16 [512, 512], replicated, may hold values from -0.25 to 0.25
- w_e2: bfloat16 [512, 512], replicated, may hold values from -0.25 to 0.25
- w_node: bfloat16 [1024, 512], replicated, may hold values from -0.1875 to 0.1875
- w_out: bfloat16 [512, 227], replicated, may hold values from -0.25 to 0.25
- bias_edge: float32 [512], replicated, may hold values from -3 to 3
- bias_node: float32 [512], replicated, may hold values from -3 to 3
Outputs:
- grid_grad: float32 [64, 4, 256, 512], P('lat', 'lon')
- mesh_grad: float32 [256, 64, 512], P('lat', 'lon')
- grad_em: float32 [512, 512], P('lat')
- grad_eg: float32 [512, 512], P('lat')
- grad_e2: float32 [512, 512], P('lat')
- grad_node: float32 [1024, 512], P('lat')
- grad_out: float32 [512, 227], P('lat')
The draws below stay inside these ranges and needn't reach their ends.
Inputs may be any that keep to these rules, and one draw needn't show every extreme that they name: `neighbours`: slots count row by row over (6) x (18) slots; a point's three slots are some slot s, s + 1 and s + 18. Points 0 to live - 1 of a tile are real, the others padding.
All inputs are finite; a program needn't handle non-finite values.
Results may differ from the reference program's by a relative error of at most 0.018.
Values may be sent and summed in bfloat16 or wider, within the bound.
No kernel may reach another device: no remote copies, remote signals or barrier semaphores. Data moves between devices by JAX's collectives and lax.ppermute only.
A program may use at most 64 MiB of HBM per device.

```python
import jax
import jax.numpy as jnp
from jax import lax

D = 512
CH = 227
P_DEV = 256
ML = 4
MO = 16
NML = 256
NMO = 64
N_LAT = 64
N_LON = 4


def draw_neighbours(key, part):
    key_row, key_col = jax.random.split(jax.random.fold_in(key, 11))
    base_row = jax.random.randint(key_row, (N_LAT, N_LON, P_DEV), 0, ML + 1, dtype=jnp.int32)
    base_col = jax.random.randint(key_col, (N_LAT, N_LON, P_DEV), 0, MO + 1, dtype=jnp.int32)
    base_row = base_row.at[:, :, 0].set(ML).at[:, :, 1].set(0)
    base_col = base_col.at[:, :, 0].set(MO).at[:, :, 1].set(0)
    slot_width = MO + 2
    first = base_row * slot_width + base_col
    return jnp.stack([first, first + 1, first + slot_width], axis=2).astype(jnp.int32)


def draw_live(key, part):
    key_count, key_place = jax.random.split(jax.random.fold_in(key, 23))
    counts = jax.random.randint(key_count, (N_LAT * N_LON,), P_DEV // 4, P_DEV + 1, dtype=jnp.int32)
    place = jax.random.randint(key_place, (), 0, N_LAT * N_LON, dtype=jnp.int32)
    counts = counts.at[place].set(P_DEV)
    counts = counts.at[(place + 1) % (N_LAT * N_LON)].set(P_DEV // 4)
    return counts.reshape(N_LAT, N_LON).astype(jnp.int32)


def block_scale(rng, dims, cuts, least, largest):
    def one(dim, blocks):
        heights = jax.random.uniform(jax.random.fold_in(jax.random.fold_in(rng, 6), dim), (blocks,), jnp.float32, least / len(cuts), largest / len(cuts))
        return jnp.repeat(jnp.exp(heights), dims[dim] // blocks).reshape((-1,) + (1,) * (len(dims) - dim - 1))

    gain = one(*cuts[0])
    for cut in cuts[1:]:
        gain = gain * one(*cut)
    return gain


def gaussian(key, shape, spread, limit, cuts=(), held_as=jnp.bfloat16):
    loudness = block_scale(key, shape, cuts, -0.22, 0.18) if cuts else 1.0
    drawn = jax.random.normal(key, shape, jnp.float32) * spread * loudness
    return jnp.minimum(jnp.maximum(drawn, -limit), limit).astype(held_as)


def setup_inputs(seed: int = 0) -> dict:
    splits = jax.random.split(jax.random.key(seed), 13)
    grid_latent = gaussian(splits[0], (N_LAT, N_LON, P_DEV, D), 1.0, 6.0, ((0, 64), (1, 4)))
    mesh_latent = gaussian(splits[1], (NML, NMO, D), 1.0, 6.0, ((0, 64), (1, 4)))
    cotangent = gaussian(splits[2], (N_LAT, N_LON, P_DEV, CH), 1.0, 6.0, ((0, 64), (1, 4)))
    neighbours = draw_neighbours(jax.random.fold_in(splits[12], 71), 0)
    live = draw_live(jax.random.fold_in(splits[12], 71), 0)
    w_em = gaussian(splits[5], (D, D), D ** -0.5, 0.25)
    w_eg = gaussian(splits[6], (D, D), D ** -0.5, 0.25)
    w_e2 = gaussian(splits[7], (D, D), D ** -0.5, 0.25)
    w_node = gaussian(splits[8], (2 * D, D), (2 * D) ** -0.5, 0.1875)
    w_out = gaussian(splits[9], (D, CH), D ** -0.5, 0.25)
    bias_edge = gaussian(splits[10], (D,), 0.5, 3.0, (), jnp.float32)
    bias_node = gaussian(splits[11], (D,), 0.5, 3.0, (), jnp.float32)
    return dict(grid_latent=grid_latent, mesh_latent=mesh_latent, cotangent=cotangent, neighbours=neighbours, live=live, w_em=w_em, w_eg=w_eg, w_e2=w_e2, w_node=w_node, w_out=w_out, bias_edge=bias_edge, bias_node=bias_node)


def silu_grad(values):
    sigma = jax.nn.sigmoid(values)
    return sigma * (1.0 + values * (1.0 - sigma))

def reference(grid_latent, mesh_latent, cotangent, neighbours, live, w_em, w_eg, w_e2, w_node, w_out, bias_edge, bias_node):
    nodes_all = NML * NMO
    slot_width = MO + 2
    mesh_flat = mesh_latent.reshape(nodes_all, D)
    projected = jnp.dot(mesh_flat, w_em, preferred_element_type=jnp.float32)
    lon_index = lax.iota(jnp.int32, N_LON)
    point_index = lax.iota(jnp.int32, P_DEV)
    zero_bf = jnp.zeros((), jnp.bfloat16)

    def lat_block(running, inputs):
        sums, node_total = running
        lat_index, grid_rows, slot_ids, counts, cot_rows = inputs
        slot_row = slot_ids // slot_width
        slot_col = slot_ids % slot_width
        node_row = lat_index * ML + slot_row - 1
        node_col = (lon_index[:, None, None] * MO + slot_col - 1) % NMO
        valid = (node_row >= 0) & (node_row < NML)
        node_ids = jnp.where(valid, node_row * NMO + node_col, 0).astype(jnp.int32)
        node_ids = jnp.transpose(node_ids, (1, 0, 2)).reshape(3, N_LON * P_DEV)
        valid = jnp.transpose(valid, (1, 0, 2)).reshape(3, N_LON * P_DEV)
        flat_grid = grid_rows.reshape(N_LON * P_DEV, D)
        grid_proj = jnp.dot(flat_grid, w_eg, preferred_element_type=jnp.float32) + bias_edge
        edge_pre = jnp.where(valid[..., None], projected[node_ids], jnp.zeros((), jnp.float32)) + grid_proj[None]
        edge_hidden = jax.nn.silu(edge_pre).astype(jnp.bfloat16)
        aggregate = jnp.einsum('kpi,ij->pj', edge_hidden.astype(jnp.float32), w_e2.astype(jnp.float32)).astype(jnp.bfloat16)
        node_pre = jnp.dot(flat_grid, w_node[:D], preferred_element_type=jnp.float32) + jnp.dot(aggregate, w_node[D:], preferred_element_type=jnp.float32) + bias_node
        node_hidden = jax.nn.silu(node_pre).astype(jnp.bfloat16)
        point_mask = (point_index[None, :] < counts[:, None]).reshape(-1)
        out_grad = jnp.where(point_mask[:, None], cot_rows.reshape(N_LON * P_DEV, CH), zero_bf)
        node_grad = (jnp.dot(out_grad, w_out.T, preferred_element_type=jnp.float32) * silu_grad(node_pre)).astype(jnp.bfloat16)
        part_out = jnp.dot(node_hidden.T, out_grad, preferred_element_type=jnp.float32)
        part_node = jnp.concatenate([jnp.dot(flat_grid.T, node_grad, preferred_element_type=jnp.float32), jnp.dot(aggregate.T, node_grad, preferred_element_type=jnp.float32)], axis=0)
        agg_grad = jnp.dot(node_grad, w_node[D:].T, preferred_element_type=jnp.float32).astype(jnp.bfloat16)
        part_e2 = jnp.einsum('kpi,pj->ij', edge_hidden.astype(jnp.float32), agg_grad.astype(jnp.float32))
        hidden_grad = jnp.dot(agg_grad, w_e2.T, preferred_element_type=jnp.float32)
        edge_grad = (hidden_grad[None] * silu_grad(edge_pre)).astype(jnp.bfloat16)
        edge_sum = lax.optimization_barrier(jnp.sum(edge_grad.astype(jnp.float32), axis=0)).astype(jnp.bfloat16)
        part_eg = jnp.dot(flat_grid.T, edge_sum, preferred_element_type=jnp.float32)
        grid_grad = jnp.dot(node_grad, w_node[:D].T, preferred_element_type=jnp.float32) + jnp.dot(edge_sum, w_eg.T, preferred_element_type=jnp.float32)
        contrib = jnp.where(valid[..., None], edge_grad.astype(jnp.float32), jnp.zeros((), jnp.float32))
        node_part = jax.ops.segment_sum(contrib.reshape(3 * N_LON * P_DEV, D), node_ids.reshape(-1), num_segments=nodes_all)
        sums = (sums[0] + part_eg, sums[1] + part_e2, sums[2] + part_node, sums[3] + part_out)
        return ((sums, node_total + node_part), grid_grad.reshape(N_LON, P_DEV, D))
    init_sums = (jnp.zeros((D, D), jnp.float32), jnp.zeros((D, D), jnp.float32), jnp.zeros((2 * D, D), jnp.float32), jnp.zeros((D, CH), jnp.float32))
    init_nodes = jnp.zeros((nodes_all, D), jnp.float32)
    lat_ids = lax.iota(jnp.int32, N_LAT)
    (sums, node_total), grid_grads = lax.scan(lat_block, (init_sums, init_nodes), (lat_ids, grid_latent, neighbours, live, cotangent))
    node_sum = node_total.astype(jnp.bfloat16)
    mesh_grad = jnp.dot(node_sum, w_em.T, preferred_element_type=jnp.float32).reshape(NML, NMO, D)
    grad_em = jnp.dot(mesh_flat.T, node_sum, preferred_element_type=jnp.float32)
    return (grid_grads, mesh_grad, grad_em, sums[0], sums[1], sums[2], sums[3])
```

```python
import functools

import jax
import jax.numpy as jnp
from jax import lax
from jax.experimental import pallas as pl
from jax.experimental.pallas import tpu as pltpu
from jax.sharding import Mesh
from jax.sharding import PartitionSpec as P

D = 512
CH = 227
LAT = ("y_lo", "z", "x")
LON = ("y_hi", "core")
SIZES = {"y_lo": 2, "z": 8, "x": 4, "y_hi": 2, "core": 2}
F32 = jnp.float32
BF = jnp.bfloat16
PANELS = 11


def mm(a, b):
    return lax.dot_general(a, b, (((1,), (0,)), ((), ())), preferred_element_type=F32)


def mm_nt(a, b):
    return lax.dot_general(a, b, (((1,), (1,)), ((), ())), preferred_element_type=F32)


def mm_tn(a, b):
    return lax.dot_general(a, b, (((0,), (0,)), ((), ())), preferred_element_type=F32)


def split(value):
    high = value.astype(BF)
    return high, (value - high.astype(F32)).astype(BF)


def halves(ref, value):
    width = value.shape[1] // 2
    ref[0] = value[:, :width].astype(ref.dtype)
    ref[1] = value[:, width:].astype(ref.dtype)


def main_kernel(
    live_ref,
    core_ref,
    nbr_ref,
    g_ref,
    ext_ref,
    cot_ref,
    w_em_ref,
    w_eg_ref,
    w_e2_ref,
    w_node_ref,
    w_out_ref,
    b_edge_ref,
    b_node_ref,
    grid_ref,
    slot_ref,
    keep_ref,
    send_ref,
    og_ref,
    wo_ref,
    ng_half,
    og_half,
    ag_half,
    es_half,
    sl_half,
    slope_ref,
):
    core = core_ref[0]
    g = g_ref[...]
    ext = ext_ref[...]
    points = g.shape[0]
    og_ref[...] = jnp.zeros_like(og_ref)
    wo_ref[...] = jnp.zeros_like(wo_ref)
    row = lax.broadcasted_iota(jnp.int32, (points, CH), 0)
    cot = cot_ref[...]
    og_ref[:, :CH] = jnp.where(row < live_ref[0], cot, jnp.zeros_like(cot))
    wo_ref[:, :CH] = w_out_ref[...]
    out_grad = og_ref[...]
    halves(og_half, out_grad)

    projected = mm(ext, w_em_ref[...])
    high, low = split(projected)
    both = jnp.concatenate([high, low], axis=0)
    grid_proj = mm(g, w_eg_ref[...]) + b_edge_ref[...]
    place = lax.broadcasted_iota(jnp.int32, (128, points), 0)
    hidden_sum = None
    hots = []
    for k in range(3):
        slot = nbr_ref[k : k + 1, :]
        r = (slot * 3641) >> 16
        c = slot - r * 18
        inner = jnp.where(
            c == 0, 99 + r, jnp.where(c == 17, 103 + r, (r - 1) * 16 + c - 1)
        )
        where = jnp.where(r == 0, 64 + c, jnp.where(r == 5, 82 + c, inner))
        hot = jnp.where(place == where, 1.0, 0.0).astype(BF)
        hots.append(hot)
        pre = mm_tn(jnp.concatenate([hot, hot], axis=0), both) + grid_proj
        sigma = jax.nn.sigmoid(pre)
        hidden = (pre * sigma).astype(BF)
        slope_ref[k] = sigma * (1.0 + pre * (1.0 - sigma))
        hidden = hidden.astype(F32)
        hidden_sum = hidden if hidden_sum is None else hidden_sum + hidden
    hs_high, hs_low = split(hidden_sum)
    aggregate = (mm(hs_high, w_e2_ref[...]) + mm(hs_low, w_e2_ref[...])).astype(BF)
    node_pre = mm(g, w_node_ref[:D, :]) + mm(aggregate, w_node_ref[D:, :]) + b_node_ref[...]
    sigma = jax.nn.sigmoid(node_pre)
    node_hidden = (node_pre * sigma).astype(BF)
    node_grad = (mm_nt(out_grad, wo_ref[...]) * (sigma * (1.0 + node_pre * (1.0 - sigma)))).astype(
        BF
    )
    halves(ng_half, node_grad)
    agg_grad = mm_nt(node_grad, w_node_ref[D:, :]).astype(BF)
    halves(ag_half, agg_grad)
    hidden_grad = mm_nt(agg_grad, w_e2_ref[...])
    edge_sum = None
    slots = None
    for k in range(3):
        edge_grad = (hidden_grad * slope_ref[k]).astype(BF)
        part = mm(hots[k], edge_grad)
        slots = part if slots is None else slots + part
        edge_grad = edge_grad.astype(F32)
        edge_sum = edge_grad if edge_sum is None else edge_sum + edge_grad
    edge_sum = edge_sum.astype(BF)
    halves(es_half, edge_sum)
    slot_ref[...] = slots
    sl_high, sl_low = split(slots)
    halves(sl_half, jnp.concatenate([sl_high, sl_low], axis=0))
    grid_ref[...] = mm_nt(node_grad, w_node_ref[:D, :]) + mm_nt(edge_sum, w_eg_ref[...])

    def put(ref, panel, value):
        v = value.reshape(16, 4, 8, 128)
        for x in range(4):
            ref[panel, x] = v[:, x].reshape(128, 128).astype(BF)

    def put_wide(ref, panel, value):
        put(ref, panel, value[:, :128])
        put(ref, panel + 1, value[:, 128:])

    ext_both = jnp.concatenate([ext, ext], axis=0)
    for ref, which in ((send_ref, 1 - core), (keep_ref, core)):
        put_wide(ref, 0, mm_tn(ext_both, sl_half[which]))
        put_wide(ref, 2, mm_tn(g, es_half[which]))
        ag = ag_half[which]
        put_wide(ref, 4, mm_tn(hs_high, ag) + mm_tn(hs_low, ag))
        ng = ng_half[which]
        for half, left in enumerate((g, aggregate)):
            value = mm_tn(left, ng)
            v = value.reshape(8, 4, 2, 8, 256)
            for x in range(4):
                for eight in range(2):
                    tile = v[:, x, eight].reshape(64, 256).astype(BF)
                    for wide in range(2):
                        ref[6 + 2 * eight + wide, x, half * 64 : half * 64 + 64, :] = tile[
                            :, wide * 128 : wide * 128 + 128
                        ]
        put(ref, 10, mm_tn(node_hidden, og_half[which]))


def vmem(n):
    return [pl.BlockSpec(memory_space=pltpu.VMEM)] * n


def smem(n):
    return [pl.BlockSpec(memory_space=pltpu.SMEM)] * n


PARAMS = pltpu.CompilerParams(vmem_limit_bytes=48 * 1024 * 1024)


def main_call(live, core, nbr, g, ext, cot, *weights):
    shape = jax.ShapeDtypeStruct
    return pl.pallas_call(
        main_kernel,
        out_shape=(
            shape((256, D), F32),
            shape((128, D), F32),
            shape((PANELS, 4, 128, 128), BF),
            shape((PANELS, 4, 128, 128), BF),
        ),
        in_specs=smem(2) + vmem(11),
        out_specs=tuple(vmem(4)),
        scratch_shapes=[
            pltpu.VMEM((256, 256), BF),
            pltpu.VMEM((D, 256), BF),
            pltpu.VMEM((2, 256, 256), BF),
            pltpu.VMEM((2, 256, 128), BF),
            pltpu.VMEM((2, 256, 256), BF),
            pltpu.VMEM((2, 256, 256), BF),
            pltpu.VMEM((2, 256, 256), BF),
            pltpu.VMEM((3, 256, D), F32),
        ],
        compiler_params=PARAMS,
        name="decoder_grads",
    )(live, core, nbr, g, ext, cot, *weights)


def core_sum_kernel(x_ref, keep_ref, got_ref, own_ref, *sends):
    x = x_ref[0]
    own_ref[...] = keep_ref[:, x].astype(F32) + got_ref[:, x].astype(F32)
    for step, ref in enumerate(sends):
        to = (x + step + 1) & 3
        ref[...] = (keep_ref[:, to].astype(F32) + got_ref[:, to].astype(F32)).astype(BF)


def core_sum(x, keep, got):
    shape = jax.ShapeDtypeStruct
    part = (PANELS, 128, 128)
    return pl.pallas_call(
        core_sum_kernel,
        out_shape=(shape(part, F32),) + (shape(part, BF),) * 3,
        in_specs=smem(1) + vmem(2),
        out_specs=tuple(vmem(4)),
        compiler_params=PARAMS,
        name="sum_over_core",
    )(x, keep, got)


def x_sum_kernel(own_ref, a_ref, b_ref, c_ref, out_ref):
    total = own_ref[...] + a_ref[...].astype(F32) + b_ref[...].astype(F32) + c_ref[...].astype(F32)
    total = total.reshape(PANELS, 16, 8, 128)
    for i in range(16):
        out_ref[i] = total[:, i].reshape(PANELS * 8, 128).astype(BF)


def x_sum(own, a, b, c):
    return pl.pallas_call(
        x_sum_kernel,
        out_shape=jax.ShapeDtypeStruct((16, PANELS * 8, 128), BF),
        in_specs=vmem(4),
        out_specs=vmem(1)[0],
        compiler_params=PARAMS,
        name="sum_over_x",
    )(own, a, b, c)


def last_kernel(in_ref, em_ref, eg_ref, e2_ref, node_ref, out_ref):
    for core in range(2):
        total = in_ref[core].astype(F32) + in_ref[core + 2].astype(F32)

        def panel(i):
            return total[8 * i : 8 * i + 8, :]

        for wide in range(2):
            at = slice((2 * core + wide) * 128, (2 * core + wide) * 128 + 128)
            em_ref[:, at] = panel(wide)
            eg_ref[:, at] = panel(2 + wide)
            e2_ref[:, at] = panel(4 + wide)
            node_ref[:8, at] = panel(6 + wide)
            node_ref[8:, at] = panel(8 + wide)
        if core == 0:
            out_ref[:, :128] = panel(10)
        else:
            out_ref[:, 128:] = panel(10)[:, : CH - 128]


def last(gathered):
    shape = jax.ShapeDtypeStruct
    return pl.pallas_call(
        last_kernel,
        out_shape=(
            shape((8, D), F32),
            shape((8, D), F32),
            shape((8, D), F32),
            shape((16, D), F32),
            shape((8, CH), F32),
        ),
        in_specs=vmem(1),
        out_specs=tuple(vmem(5)),
        compiler_params=PARAMS,
        name="sum_over_lon",
    )(gathered)


def shift(value, axes, steps, wrap):
    size = 1
    for a in axes:
        size *= SIZES[a]
    pairs = [(i, (i + steps) % size) for i in range(size) if wrap or 0 <= i + steps < size]
    return lax.ppermute(value, axes, pairs)


def on_device(
    grid_latent,
    mesh_latent,
    cotangent,
    neighbours,
    live,
    w_em,
    w_eg,
    w_e2,
    w_node,
    w_out,
    bias_edge,
    bias_node,
):
    west = shift(mesh_latent[:, 15], LON, 1, True)
    east = shift(mesh_latent[:, 0], LON, -1, True)
    top = jnp.concatenate([west[:1], mesh_latent[0], east[:1]], axis=0)
    bottom = jnp.concatenate([west[3:], mesh_latent[3], east[3:]], axis=0)
    north = shift(bottom, LAT, 1, False)
    south = shift(top, LAT, -1, False)
    ext = jnp.concatenate(
        [mesh_latent.reshape(64, D), north, south, west, east, jnp.zeros((20, D), BF)], axis=0
    )
    core = lax.axis_index("core").astype(jnp.int32).reshape(1)
    x = lax.axis_index("x").astype(jnp.int32).reshape(1)
    grid_grad, slots, keep, send = main_call(
        live.reshape(1),
        core,
        neighbours[0, 0],
        grid_latent[0, 0],
        ext,
        cotangent[0, 0],
        w_em,
        w_eg,
        w_e2,
        w_node,
        w_out,
        bias_edge.reshape(1, D),
        bias_node.reshape(1, D),
    )
    got = lax.ppermute(send, "core", [(0, 1), (1, 0)])
    own, *sends = core_sum(x, keep, got)
    came = [
        lax.ppermute(part, "x", [(i, (i + step + 1) % 4) for i in range(4)])
        for step, part in enumerate(sends)
    ]
    chunks = x_sum(own, *came)
    chunks = lax.all_to_all(chunks, ("y_lo", "z"), 0, 0, tiled=True)
    part = jnp.sum(chunks.astype(F32), axis=0).astype(BF)
    gathered = lax.all_gather(part, LON, axis=0, tiled=False)
    grads = last(gathered)

    from_south = shift(slots[64:82].astype(BF), LAT, -1, False).astype(F32)
    from_north = shift(slots[82:100].astype(BF), LAT, 1, False).astype(F32)
    to_west = slots[100:104].at[3].add(from_south[0]).at[0].add(from_north[0])
    to_east = slots[104:108].at[3].add(from_south[17]).at[0].add(from_north[17])
    from_east = shift(to_west.astype(BF), LON, -1, True).astype(F32)
    from_west = shift(to_east.astype(BF), LON, 1, True).astype(F32)
    owned = slots[:64].reshape(4, 16, D)
    owned = owned.at[3].add(from_south[1:17]).at[0].add(from_north[1:17])
    owned = owned.at[:, 15].add(from_east).at[:, 0].add(from_west)
    node_sum = owned.reshape(64, D).astype(BF)
    mesh_grad = mm_nt(node_sum, w_em).reshape(4, 16, D)
    return (grid_grad.reshape(1, 1, 256, D), mesh_grad) + tuple(grads)


def solution(mesh):
    fine = Mesh(mesh.devices.reshape(tuple(SIZES.values())), tuple(SIZES))
    in_specs = (
        P(LAT, LON, None, None),
        P(LAT, LON, None),
        P(LAT, LON, None, None),
        P(LAT, LON, None, None),
        P(LAT, LON),
    ) + (P(),) * 7
    out_specs = (P(LAT, LON, None, None), P(LAT, LON, None)) + (P(LAT, None),) * 5
    return jax.shard_map(
        on_device, mesh=fine, in_specs=in_specs, out_specs=out_specs, check_vma=False
    )
```

```python
import jax
import jax.numpy as jnp
from jax import lax
from jax.experimental import pallas as pl
from jax.experimental.pallas import tpu as pltpu
from jax.sharding import Mesh
from jax.sharding import PartitionSpec as P

D = 512
CH = 227
LAT = ("y_lo", "z", "x")
LON = ("y_hi", "core")
SIZES = {"y_lo": 2, "z": 8, "x": 4, "y_hi": 2, "core": 2}
F32 = jnp.float32
BF = jnp.bfloat16
PANELS = 11


def mm(a, b):
    return lax.dot_general(a, b, (((1,), (0,)), ((), ())), preferred_element_type=F32)


def mm_nt(a, b):
    return lax.dot_general(a, b, (((1,), (1,)), ((), ())), preferred_element_type=F32)


def mm_tn(a, b):
    return lax.dot_general(a, b, (((0,), (0,)), ((), ())), preferred_element_type=F32)


def split(value):
    high = value.astype(BF)
    return high, (value - high.astype(F32)).astype(BF)


def halves(ref, value):
    width = value.shape[1] // 2
    ref[0] = value[:, :width].astype(ref.dtype)
    ref[1] = value[:, width:].astype(ref.dtype)


W_EM, W_EG, W_E2, W_NODE, GRID, MESH, W_OUT = (0, 512, 1024, 1536, 2560, 2816, 2880)


def main_kernel(
    place_ref,
    north_ref,
    south_ref,
    mate_ref,
    opposite_ref,
    pack_ref,
    bias_ref,
    cot_ref,
    core_ref,
    grid_ref,
    slot_ref,
    keep_ref,
    send_ref,
    ext_ref,
    ng_half,
    og_half,
    ag_half,
    es_half,
    sl_half,
    slope_ref,
    og_ref,
):
    w_em_ref = pack_ref.at[W_EM:W_EG]
    w_eg_ref = pack_ref.at[W_EG:W_E2]
    w_e2_ref = pack_ref.at[W_E2:W_NODE]
    w_node_ref = pack_ref.at[W_NODE:GRID]
    g_ref = pack_ref.at[GRID:MESH]
    mesh_ref = pack_ref.at[MESH:W_OUT]
    wo_ref = pack_ref.at[W_OUT : W_OUT + 256]
    core = core_ref[0]
    points = 256
    ext_ref[:64, :] = mesh_ref[...].astype(F32)
    ext_ref[64:, :] = jnp.zeros((64, D), F32)
    ext_ref[64:82, :] = north_ref[...].astype(F32)
    ext_ref[88:106, :] = south_ref[...].astype(F32)
    ext_ref[112:116, :] = mate_ref[...].astype(F32)
    ext_ref[120:124, :] = opposite_ref[...].astype(F32)
    ext = ext_ref[...].astype(BF)
    row = lax.broadcasted_iota(jnp.int32, (128, points), 0)
    hots = [jnp.where(row == place_ref[k : k + 1, :], 1.0, 0.0).astype(BF) for k in range(3)]
    g = g_ref[...]
    projected = mm(ext, w_em_ref[...])
    high, low = split(projected)
    both = jnp.concatenate([high, low], axis=0)
    grid_proj = mm(g, w_eg_ref[...]) + bias_ref[0:1, :]
    hidden_sum = None
    for k in range(3):
        pre = mm_tn(jnp.concatenate([hots[k], hots[k]], axis=0), both) + grid_proj
        sigma = jax.nn.sigmoid(pre)
        hidden = (pre * sigma).astype(BF)
        slope_ref[k] = sigma * (1.0 + pre * (1.0 - sigma))
        hidden = hidden.astype(F32)
        hidden_sum = hidden if hidden_sum is None else hidden_sum + hidden
    hs_high, hs_low = split(hidden_sum)
    og_ref[...] = jnp.zeros_like(og_ref)
    og_ref[:CH, :] = cot_ref[...]
    out_grad = og_ref[...].T
    halves(og_half, out_grad)

    aggregate = (mm(hs_high, w_e2_ref[...]) + mm(hs_low, w_e2_ref[...])).astype(BF)
    node_pre = mm(g, w_node_ref[:D, :]) + mm(aggregate, w_node_ref[D:, :]) + bias_ref[1:2, :]
    sigma = jax.nn.sigmoid(node_pre)
    node_hidden = (node_pre * sigma).astype(BF)
    node_grad = (mm(out_grad, wo_ref[...]) * (sigma * (1.0 + node_pre * (1.0 - sigma)))).astype(BF)
    halves(ng_half, node_grad)
    agg_grad = mm_nt(node_grad, w_node_ref[D:, :]).astype(BF)
    halves(ag_half, agg_grad)
    hidden_grad = mm_nt(agg_grad, w_e2_ref[...])
    edge_sum = None
    slots = None
    for k in range(3):
        edge_grad = (hidden_grad * slope_ref[k]).astype(BF)
        part = mm(hots[k], edge_grad)
        slots = part if slots is None else slots + part
        edge_grad = edge_grad.astype(F32)
        edge_sum = edge_grad if edge_sum is None else edge_sum + edge_grad
    edge_sum = edge_sum.astype(BF)
    halves(es_half, edge_sum)
    slot_ref[...] = slots
    sl_high, sl_low = split(slots)
    halves(sl_half, jnp.concatenate([sl_high, sl_low], axis=0))
    grid_ref[...] = mm_nt(node_grad, w_node_ref[:D, :]) + mm_nt(edge_sum, w_eg_ref[...])

    def put(ref, panel, value):
        v = value.reshape(16, 4, 8, 128)
        for x in range(4):
            ref[panel, x] = v[:, x].reshape(128, 128).astype(BF)

    def put_wide(ref, panel, value):
        put(ref, panel, value[:, :128])
        put(ref, panel + 1, value[:, 128:])

    ext_both = jnp.concatenate([ext, ext], axis=0)
    for ref, which in ((send_ref, 1 - core), (keep_ref, core)):
        put_wide(ref, 0, mm_tn(ext_both, sl_half[which]))
        put_wide(ref, 2, mm_tn(g, es_half[which]))
        ag = ag_half[which]
        put_wide(ref, 4, mm_tn(hs_high, ag) + mm_tn(hs_low, ag))
        ng = ng_half[which]
        for half, left in enumerate((g, aggregate)):
            value = mm_tn(left, ng)
            v = value.reshape(8, 4, 2, 8, 256)
            for x in range(4):
                for eight in range(2):
                    tile = v[:, x, eight].reshape(64, 256).astype(BF)
                    for wide in range(2):
                        ref[6 + 2 * eight + wide, x, half * 64 : half * 64 + 64, :] = tile[
                            :, wide * 128 : wide * 128 + 128
                        ]
        put(ref, 10, mm_tn(node_hidden, og_half[which]))


def vmem(n):
    return [pl.BlockSpec(memory_space=pltpu.VMEM)] * n


def smem(n):
    return [pl.BlockSpec(memory_space=pltpu.SMEM)] * n


def params(mebibytes):
    return pltpu.CompilerParams(vmem_limit_bytes=mebibytes * 1024 * 1024)


def main_call(*args):
    shape = jax.ShapeDtypeStruct
    return pl.pallas_call(
        main_kernel,
        out_shape=(
            shape((256, D), F32),
            shape((128, D), F32),
            shape((PANELS, 4, 128, 128), BF),
            shape((PANELS, 4, 128, 128), BF),
        ),
        in_specs=vmem(8) + smem(1),
        out_specs=tuple(vmem(4)),
        scratch_shapes=[
            pltpu.VMEM((128, D), F32),
            pltpu.VMEM((2, 256, 256), BF),
            pltpu.VMEM((2, 256, 128), BF),
            pltpu.VMEM((2, 256, 256), BF),
            pltpu.VMEM((2, 256, 256), BF),
            pltpu.VMEM((2, 256, 256), BF),
            pltpu.VMEM((3, 256, D), F32),
            pltpu.VMEM((256, 256), BF),
        ],
        compiler_params=params(28),
        name="decoder_grads",
    )(*args)


def core_sum_kernel(x_ref, keep_ref, got_ref, own_ref, *sends):
    x = x_ref[0]
    own_ref[...] = keep_ref[:, x].astype(F32) + got_ref[:, x].astype(F32)
    for step, ref in enumerate(sends):
        to = (x + step + 1) & 3
        ref[...] = (keep_ref[:, to].astype(F32) + got_ref[:, to].astype(F32)).astype(BF)


def core_sum(x, keep, got):
    shape = jax.ShapeDtypeStruct
    part = (PANELS, 128, 128)
    return pl.pallas_call(
        core_sum_kernel,
        out_shape=(shape(part, F32),) + (shape(part, BF),) * 3,
        in_specs=smem(1) + vmem(2),
        out_specs=tuple(vmem(4)),
        compiler_params=params(12),
        name="sum_over_core",
    )(x, keep, got)


def x_sum_kernel(own_ref, a_ref, b_ref, c_ref, out_ref):
    total = own_ref[...] + a_ref[...].astype(F32) + b_ref[...].astype(F32) + c_ref[...].astype(F32)
    total = total.reshape(PANELS, 16, 8, 128)
    for i in range(16):
        out_ref[i] = total[:, i].reshape(PANELS * 8, 128).astype(BF)


def x_sum(own, a, b, c):
    return pl.pallas_call(
        x_sum_kernel,
        out_shape=jax.ShapeDtypeStruct((16, PANELS * 8, 128), BF),
        in_specs=vmem(4),
        out_specs=vmem(1)[0],
        compiler_params=params(8),
        name="sum_over_x",
    )(own, a, b, c)


def last_kernel(in_ref, em_ref, eg_ref, e2_ref, node_ref, out_ref):
    for core in range(2):
        total = in_ref[core].astype(F32) + in_ref[core + 2].astype(F32)

        def panel(i):
            return total[8 * i : 8 * i + 8, :]

        for wide in range(2):
            at = slice((2 * core + wide) * 128, (2 * core + wide) * 128 + 128)
            em_ref[:, at] = panel(wide)
            eg_ref[:, at] = panel(2 + wide)
            e2_ref[:, at] = panel(4 + wide)
            node_ref[:8, at] = panel(6 + wide)
            node_ref[8:, at] = panel(8 + wide)
        if core == 0:
            out_ref[:, :128] = panel(10)
        else:
            out_ref[:, 128:] = panel(10)[:, : CH - 128]


def last(gathered):
    shape = jax.ShapeDtypeStruct
    return pl.pallas_call(
        last_kernel,
        out_shape=(
            shape((8, D), F32),
            shape((8, D), F32),
            shape((8, D), F32),
            shape((16, D), F32),
            shape((8, CH), F32),
        ),
        in_specs=vmem(1),
        out_specs=tuple(vmem(5)),
        compiler_params=params(4),
        name="sum_over_lon",
    )(gathered)


def shift(value, axes, steps):
    size = 1
    for a in axes:
        size *= SIZES[a]
    pairs = [(i, i + steps) for i in range(size) if 0 <= i + steps < size]
    return lax.ppermute(value, axes, pairs)


def to_mate(value):
    return lax.ppermute(value, "core", [(0, 1), (1, 0)])


def to_opposite(value):
    return lax.ppermute(value, LON, [(i, 3 - i) for i in range(4)])


def on_device(
    grid_latent,
    mesh_latent,
    cotangent,
    neighbours,
    live,
    w_em,
    w_eg,
    w_e2,
    w_node,
    w_out,
    bias_edge,
    bias_node,
):
    core = lax.axis_index("core").astype(jnp.int32)
    x = lax.axis_index("x").astype(jnp.int32).reshape(1)
    first, final = mesh_latent[:, 0], mesh_latent[:, 15]
    mate = to_mate(jnp.where(core == 0, final, first))
    opposite = to_opposite(jnp.where(core == 0, first, final))
    west = jnp.where(core == 0, opposite, mate)
    east = jnp.where(core == 0, mate, opposite)
    top = jnp.concatenate([west[:1], mesh_latent[0], east[:1]], axis=0)
    bottom = jnp.concatenate([west[3:], mesh_latent[3], east[3:]], axis=0)
    north = shift(bottom, LAT, 1)
    south = shift(top, LAT, -1)
    pack = jnp.concatenate(
        [w_em, w_eg, w_e2, w_node, grid_latent[0, 0], mesh_latent.reshape(64, D), w_out.T, jnp.zeros((29, D), BF)]
    )
    live_point = lax.broadcasted_iota(jnp.int32, (CH, 256), 1) < live[0, 0]
    out_grad = jnp.where(live_point, cotangent[0, 0].T, jnp.zeros((), BF))
    slot = neighbours[0, 0]
    r, c = slot // 18, slot % 18
    side = jnp.where(c == 0, 120 - 8 * core, 112 + 8 * core) + r - 1
    inner = jnp.where((c == 0) | (c == 17), side, (r - 1) * 16 + c - 1)
    place = jnp.where(r == 0, 64 + c, jnp.where(r == 5, 88 + c, inner))
    grid_grad, slots, keep, send = main_call(
        place,
        north,
        south,
        mate,
        opposite,
        pack,
        jnp.stack([bias_edge, bias_node]),
        out_grad,
        core.reshape(1),
    )
    got = lax.ppermute(send, "core", [(0, 1), (1, 0)])
    own, *sends = core_sum(x, keep, got)
    slots, sends = lax.optimization_barrier((slots, sends))
    came = [
        lax.ppermute(part, "x", [(i, (i + step + 1) % 4) for i in range(4)])
        for step, part in enumerate(sends)
    ]
    chunks = x_sum(own, *came)
    chunks = lax.all_to_all(chunks, ("y_lo", "z"), 0, 0, tiled=True)
    part = jnp.sum(chunks.astype(F32), axis=0).astype(BF)
    gathered = lax.all_gather(part, LON, axis=0, tiled=False)
    grads = last(gathered)

    from_south = shift(slots[64:82].astype(BF), LAT, -1).astype(F32)
    from_north = shift(slots[88:106].astype(BF), LAT, 1).astype(F32)
    ends = jnp.stack([from_north, jnp.zeros_like(from_north), jnp.zeros_like(from_north), from_south])
    mate = slots[112:116] + jnp.where(core == 0, ends[:, 17], ends[:, 0])
    opposite = slots[120:124] + jnp.where(core == 0, ends[:, 0], ends[:, 17])
    mate = to_mate(mate.astype(BF)).astype(F32)
    opposite = to_opposite(opposite.astype(BF)).astype(F32)
    west = jnp.where(core == 0, opposite, mate)
    east = jnp.where(core == 0, mate, opposite)
    sides = jnp.concatenate([west[:, None], jnp.zeros((4, 14, D), F32), east[:, None]], axis=1)
    owned = slots[:64].reshape(4, 16, D) + ends[:, 1:17] + sides
    node_sum = owned.reshape(64, D).astype(BF)
    mesh_grad = mm_nt(node_sum, w_em).reshape(4, 16, D)
    return (grid_grad.reshape(1, 1, 256, D), mesh_grad) + tuple(grads)


def solution(mesh):
    fine = Mesh(mesh.devices.reshape(tuple(SIZES.values())), tuple(SIZES))
    in_specs = (
        P(LAT, LON, None, None),
        P(LAT, LON, None),
        P(LAT, LON, None, None),
        P(LAT, LON, None, None),
        P(LAT, LON),
    ) + (P(),) * 7
    out_specs = (P(LAT, LON, None, None), P(LAT, LON, None)) + (P(LAT, None),) * 5
    return jax.shard_map(
        on_device, mesh=fine, in_specs=in_specs, out_specs=out_specs, check_vma=False
    )
```

```python
import jax
import jax.numpy as jnp
from jax import lax
from jax.experimental import pallas as pl
from jax.experimental.pallas import tpu as pltpu
from jax.sharding import Mesh
from jax.sharding import PartitionSpec as P

D = 512
CH = 227
LAT = ("y_lo", "z_hi", "z_lo", "x_hi", "x_lo")
LON = ("y_hi", "core")
NEAR = ("y_lo", "z_lo", "x_lo")
FAR = ("z_hi", "x_hi")
SIZES = {"y_lo": 2, "z_hi": 4, "z_lo": 2, "x_hi": 2, "x_lo": 2, "y_hi": 2, "core": 2}
F32 = jnp.float32
BF = jnp.bfloat16
PANELS = 11


def mm(a, b):
    return lax.dot_general(a, b, (((1,), (0,)), ((), ())), preferred_element_type=F32)


def mm_nt(a, b):
    return lax.dot_general(a, b, (((1,), (1,)), ((), ())), preferred_element_type=F32)


def mm_tn(a, b):
    return lax.dot_general(a, b, (((0,), (0,)), ((), ())), preferred_element_type=F32)


def split(value):
    high = value.astype(BF)
    return high, (value - high.astype(F32)).astype(BF)


def halves(ref, value):
    width = value.shape[1] // 2
    ref[0] = value[:, :width].astype(ref.dtype)
    ref[1] = value[:, width:].astype(ref.dtype)


def main_kernel(
    core_ref,
    live_ref,
    bias_ref,
    place_ref,
    pair_hbm,
    other_hbm,
    mate_hbm,
    opposite_hbm,
    mesh_hbm,
    w_em_hbm,
    g_hbm,
    w_eg_hbm,
    w_e2_hbm,
    w_node_hbm,
    cot_hbm,
    w_out_hbm,
    grid_ref,
    slot_ref,
    keep_ref,
    send_ref,
    pair_ref,
    other_ref,
    mate_ref,
    opposite_ref,
    mesh_ref,
    w_em_ref,
    g_ref,
    w_eg_ref,
    w_e2_ref,
    w_node_ref,
    cot_ref,
    w_out_ref,
    sems,
    ext_ref,
    ng_half,
    og_half,
    ag_half,
    es_half,
    sl_half,
    slope_ref,
    og_ref,
    wo_ref,
):
    ways = (
        (mesh_hbm, mesh_ref),
        (pair_hbm, pair_ref),
        (other_hbm, other_ref),
        (mate_hbm, mate_ref),
        (opposite_hbm, opposite_ref),
        (w_em_hbm, w_em_ref),
        (g_hbm, g_ref),
        (w_eg_hbm, w_eg_ref),
        (w_e2_hbm, w_e2_ref),
        (w_node_hbm, w_node_ref),
        (cot_hbm, cot_ref),
        (w_out_hbm, w_out_ref),
    )
    copies = [pltpu.make_async_copy(a, b, sems.at[i]) for i, (a, b) in enumerate(ways)]
    for copy in copies:
        copy.start()
    core = core_ref[0]
    points = 256
    ext_ref[64:, :] = jnp.zeros((64, D), F32)
    for copy in copies[:5]:
        copy.wait()
    ext_ref[:64, :] = mesh_ref[...].astype(F32)
    ext_ref[64:82, :] = pair_ref[...].astype(F32)
    ext_ref[88:106, :] = other_ref[...].astype(F32)
    ext_ref[112:116, :] = mate_ref[...].astype(F32)
    ext_ref[120:124, :] = opposite_ref[...].astype(F32)
    ext = ext_ref[...].astype(BF)
    row = lax.broadcasted_iota(jnp.int32, (128, points), 0)
    hots = [jnp.where(row == place_ref[k : k + 1, :], 1.0, 0.0).astype(BF) for k in range(3)]
    copies[5].wait()
    projected = mm(ext, w_em_ref[...])
    high, low = split(projected)
    both = jnp.concatenate([high, low], axis=0)
    copies[6].wait()
    copies[7].wait()
    g = g_ref[...]
    grid_proj = mm(g, w_eg_ref[...]) + bias_ref[0:1, :]
    hidden_sum = None
    for k in range(3):
        pre = mm_tn(jnp.concatenate([hots[k], hots[k]], axis=0), both) + grid_proj
        sigma = jax.nn.sigmoid(pre)
        hidden = (pre * sigma).astype(BF)
        slope_ref[k] = sigma * (1.0 + pre * (1.0 - sigma))
        hidden = hidden.astype(F32)
        hidden_sum = hidden if hidden_sum is None else hidden_sum + hidden
    hs_high, hs_low = split(hidden_sum)
    for copy in copies[8:]:
        copy.wait()
    og_ref[...] = jnp.zeros_like(og_ref)
    wo_ref[...] = jnp.zeros_like(wo_ref)
    column = lax.broadcasted_iota(jnp.int32, (CH, points), 1)
    cot = cot_ref[...]
    og_ref[:CH, :] = jnp.where(column < live_ref[0], cot, jnp.zeros_like(cot))
    wo_ref[:CH, :] = w_out_ref[...]
    out_grad = og_ref[...].T
    halves(og_half, out_grad)

    aggregate = (mm(hs_high, w_e2_ref[...]) + mm(hs_low, w_e2_ref[...])).astype(BF)
    node_pre = mm(g, w_node_ref[:D, :]) + mm(aggregate, w_node_ref[D:, :]) + bias_ref[1:2, :]
    sigma = jax.nn.sigmoid(node_pre)
    node_hidden = (node_pre * sigma).astype(BF)
    node_grad = (mm(out_grad, wo_ref[...]) * (sigma * (1.0 + node_pre * (1.0 - sigma)))).astype(BF)
    halves(ng_half, node_grad)
    agg_grad = mm_nt(node_grad, w_node_ref[D:, :]).astype(BF)
    halves(ag_half, agg_grad)
    hidden_grad = mm_nt(agg_grad, w_e2_ref[...])
    edge_sum = None
    slots = None
    for k in range(3):
        edge_grad = (hidden_grad * slope_ref[k]).astype(BF)
        part = mm(hots[k], edge_grad)
        slots = part if slots is None else slots + part
        edge_grad = edge_grad.astype(F32)
        edge_sum = edge_grad if edge_sum is None else edge_sum + edge_grad
    edge_sum = edge_sum.astype(BF)
    halves(es_half, edge_sum)
    slot_ref[...] = slots
    sl_high, sl_low = split(slots)
    halves(sl_half, jnp.concatenate([sl_high, sl_low], axis=0))
    grid_ref[...] = mm_nt(node_grad, w_node_ref[:D, :]) + mm_nt(edge_sum, w_eg_ref[...])

    def put(ref, panel, value):
        v = value.reshape(2, 4, 2, 2, 2, 8, 128)
        for i in range(8):
            tile = v[i >> 2, :, (i >> 1) & 1, :, i & 1]
            ref[panel, i] = tile.reshape(64, 128).astype(BF)

    def put_wide(ref, panel, value):
        put(ref, panel, value[:, :128])
        put(ref, panel + 1, value[:, 128:])

    ext_both = jnp.concatenate([ext, ext], axis=0)
    for ref, which in ((send_ref, 1 - core), (keep_ref, core)):
        put_wide(ref, 0, mm_tn(ext_both, sl_half[which]))
        put_wide(ref, 2, mm_tn(g, es_half[which]))
        ag = ag_half[which]
        put_wide(ref, 4, mm_tn(hs_high, ag) + mm_tn(hs_low, ag))
        ng = ng_half[which]
        for half, left in enumerate((g, aggregate)):
            v = mm_tn(left, ng).reshape(4, 2, 2, 2, 2, 8, 256)
            for i in range(4):
                for eight in range(2):
                    tile = v[:, i >> 1, :, i & 1, eight].reshape(64, 256).astype(BF)
                    for wide in range(2):
                        ref[6 + 2 * eight + wide, 4 * half + i] = tile[:, wide * 128 : wide * 128 + 128]
        put(ref, 10, mm_tn(node_hidden, og_half[which]))


def vmem(n):
    return [pl.BlockSpec(memory_space=pltpu.VMEM)] * n


def smem(n):
    return [pl.BlockSpec(memory_space=pltpu.SMEM)] * n


def params(mebibytes):
    return pltpu.CompilerParams(vmem_limit_bytes=mebibytes * 1024 * 1024)


def main_call(*args):
    shape = jax.ShapeDtypeStruct
    inputs = args[4:]
    return pl.pallas_call(
        main_kernel,
        out_shape=(
            shape((256, D), F32),
            shape((128, D), F32),
            shape((PANELS, 8, 64, 128), BF),
            shape((PANELS, 8, 64, 128), BF),
        ),
        in_specs=smem(2) + vmem(2) + [pl.BlockSpec(memory_space=pltpu.HBM)] * len(inputs),
        out_specs=tuple(vmem(4)),
        scratch_shapes=[pltpu.VMEM(a.shape, a.dtype) for a in inputs]
        + [
            pltpu.SemaphoreType.DMA((len(inputs),)),
            pltpu.VMEM((128, D), F32),
            pltpu.VMEM((2, 256, 256), BF),
            pltpu.VMEM((2, 256, 128), BF),
            pltpu.VMEM((2, 256, 256), BF),
            pltpu.VMEM((2, 256, 256), BF),
            pltpu.VMEM((2, 256, 256), BF),
            pltpu.VMEM((3, 256, D), F32),
            pltpu.VMEM((256, 256), BF),
            pltpu.VMEM((256, D), BF),
        ],
        compiler_params=params(56),
        name="decoder_grads",
    )(*args)


def core_sum_kernel(mine_ref, keep_ref, got_ref, own_ref, *sends):
    mine = mine_ref[0]
    own_ref[...] = keep_ref[:, mine].astype(F32) + got_ref[:, mine].astype(F32)
    for step, ref in enumerate(sends):
        to = mine ^ (step + 1)
        ref[...] = (keep_ref[:, to].astype(F32) + got_ref[:, to].astype(F32)).astype(BF)


def core_sum(mine, keep, got):
    shape = jax.ShapeDtypeStruct
    part = (PANELS, 64, 128)
    return pl.pallas_call(
        core_sum_kernel,
        out_shape=(shape(part, F32),) + (shape(part, BF),) * 7,
        in_specs=smem(1) + vmem(2),
        out_specs=tuple(vmem(8)),
        compiler_params=params(12),
        name="sum_over_core",
    )(mine, keep, got)


def near_sum_kernel(own_ref, *refs):
    out_ref = refs[-1]
    total = own_ref[...]
    for ref in refs[:-1]:
        total = total + ref[...].astype(F32)
    total = total.reshape(PANELS, 8, 8, 128)
    for i in range(8):
        out_ref[i] = total[:, i].reshape(PANELS * 8, 128).astype(BF)


def near_sum(own, *came):
    return pl.pallas_call(
        near_sum_kernel,
        out_shape=jax.ShapeDtypeStruct((8, PANELS * 8, 128), BF),
        in_specs=vmem(8),
        out_specs=vmem(1)[0],
        compiler_params=params(8),
        name="sum_over_near",
    )(own, *came)


def far_sum_kernel(in_ref, out_ref):
    out_ref[...] = jnp.sum(in_ref[...].astype(F32), axis=0).astype(BF)


def far_sum(chunks):
    return pl.pallas_call(
        far_sum_kernel,
        out_shape=jax.ShapeDtypeStruct((PANELS * 8, 128), BF),
        in_specs=vmem(1),
        out_specs=vmem(1)[0],
        compiler_params=params(4),
        name="sum_over_far",
    )(chunks)


def last_kernel(in_ref, em_ref, eg_ref, e2_ref, node_ref, out_ref):
    for core in range(2):
        total = in_ref[core].astype(F32) + in_ref[core + 2].astype(F32)

        def panel(i):
            return total[8 * i : 8 * i + 8, :]

        for wide in range(2):
            at = slice((2 * core + wide) * 128, (2 * core + wide) * 128 + 128)
            em_ref[:, at] = panel(wide)
            eg_ref[:, at] = panel(2 + wide)
            e2_ref[:, at] = panel(4 + wide)
            node_ref[:8, at] = panel(6 + wide)
            node_ref[8:, at] = panel(8 + wide)
        if core == 0:
            out_ref[:, :128] = panel(10)
        else:
            out_ref[:, 128:] = panel(10)[:, : CH - 128]


def last(gathered):
    shape = jax.ShapeDtypeStruct
    return pl.pallas_call(
        last_kernel,
        out_shape=(
            shape((8, D), F32),
            shape((8, D), F32),
            shape((8, D), F32),
            shape((16, D), F32),
            shape((8, CH), F32),
        ),
        in_specs=vmem(1),
        out_specs=tuple(vmem(5)),
        compiler_params=params(4),
        name="sum_over_lon",
    )(gathered)


def to_pair(value):
    return lax.ppermute(value, "x_lo", [(0, 1), (1, 0)])


def to_other(value):
    odd = [(i, i + 1) for i in range(1, 63, 2)]
    return lax.ppermute(value, LAT, odd + [(j, i) for i, j in odd])


def to_mate(value):
    return lax.ppermute(value, "core", [(0, 1), (1, 0)])


def to_opposite(value):
    return lax.ppermute(value, LON, [(i, 3 - i) for i in range(4)])


def on_device(
    grid_latent,
    mesh_latent,
    cotangent,
    neighbours,
    live,
    w_em,
    w_eg,
    w_e2,
    w_node,
    w_out,
    bias_edge,
    bias_node,
):
    core = lax.axis_index("core").astype(jnp.int32)
    odd = lax.axis_index("x_lo").astype(jnp.int32)
    near = lax.axis_index(NEAR).astype(jnp.int32).reshape(1)
    first, final = mesh_latent[:, 0], mesh_latent[:, 15]
    mate = to_mate(jnp.where(core == 0, final, first))
    opposite = to_opposite(jnp.where(core == 0, first, final))
    west = jnp.where(core == 0, opposite, mate)
    east = jnp.where(core == 0, mate, opposite)
    top = jnp.concatenate([west[:1], mesh_latent[0], east[:1]], axis=0)
    bottom = jnp.concatenate([west[3:], mesh_latent[3], east[3:]], axis=0)
    pair = to_pair(jnp.where(odd == 1, top, bottom))
    other = to_other(jnp.where(odd == 1, bottom, top))
    slot = neighbours[0, 0]
    r, c = slot // 18, slot % 18
    side = jnp.where(c == 0, 120 - 8 * core, 112 + 8 * core) + r - 1
    inner = jnp.where((c == 0) | (c == 17), side, (r - 1) * 16 + c - 1)
    place = jnp.where(r == 0, 88 - 24 * odd + c, jnp.where(r == 5, 64 + 24 * odd + c, inner))
    grid_grad, slots, keep, send = main_call(
        core.reshape(1),
        live.reshape(1),
        jnp.stack([bias_edge, bias_node]),
        place,
        pair,
        other,
        mate,
        opposite,
        mesh_latent.reshape(64, D),
        w_em,
        grid_latent[0, 0],
        w_eg,
        w_e2,
        w_node,
        cotangent[0, 0].T,
        w_out.T,
    )
    got = to_mate(send)
    own, *sends = core_sum(near, keep, got)
    came = [
        lax.ppermute(part, NEAR, [(i, i ^ (step + 1)) for i in range(8)])
        for step, part in enumerate(sends)
    ]
    slots, came[0] = lax.optimization_barrier((slots, came[0]))
    chunks = near_sum(own, *came)
    chunks = lax.all_to_all(chunks, FAR, 0, 0, tiled=True)
    part = far_sum(chunks)
    gathered = lax.all_gather(part, LON, axis=0, tiled=False)
    grads = last(gathered)

    pair = to_pair(slots[64:82].astype(BF)).astype(F32)
    other = to_other(slots[88:106].astype(BF)).astype(F32)
    top = jnp.where(odd == 1, pair, other)
    bottom = jnp.where(odd == 1, other, pair)
    ends = jnp.stack([top, jnp.zeros_like(top), jnp.zeros_like(top), bottom])
    mate = slots[112:116] + jnp.where(core == 0, ends[:, 17], ends[:, 0])
    opposite = slots[120:124] + jnp.where(core == 0, ends[:, 0], ends[:, 17])
    mate = to_mate(mate.astype(BF)).astype(F32)
    opposite = to_opposite(opposite.astype(BF)).astype(F32)
    west = jnp.where(core == 0, opposite, mate)
    east = jnp.where(core == 0, mate, opposite)
    sides = jnp.concatenate([west[:, None], jnp.zeros((4, 14, D), F32), east[:, None]], axis=1)
    owned = slots[:64].reshape(4, 16, D) + ends[:, 1:17] + sides
    node_sum = owned.reshape(64, D).astype(BF)
    mesh_grad = mm_nt(node_sum, w_em).reshape(4, 16, D)
    return (grid_grad.reshape(1, 1, 256, D), mesh_grad) + tuple(grads)


def solution(mesh):
    fine = Mesh(mesh.devices.reshape(tuple(SIZES.values())), tuple(SIZES))
    in_specs = (
        P(LAT, LON, None, None),
        P(LAT, LON, None),
        P(LAT, LON, None, None),
        P(LAT, LON, None, None),
        P(LAT, LON),
    ) + (P(),) * 7
    out_specs = (P(LAT, LON, None, None), P(LAT, LON, None)) + (P(LAT, None),) * 5
    return jax.shard_map(
        on_device, mesh=fine, in_specs=in_specs, out_specs=out_specs, check_vma=False
    )
```

```python
import jax
import jax.numpy as jnp
from jax import lax
from jax.experimental import pallas as pl
from jax.experimental.pallas import tpu as pltpu
from jax.sharding import Mesh
from jax.sharding import PartitionSpec as P

D = 512
CH = 227
LAT = ("y_lo", "z_hi", "z_lo", "x_hi", "x_lo")
LON = ("y_hi", "core")
NEAR = ("y_lo", "z_lo", "x_hi", "x_lo")
SIZES = {"y_lo": 2, "z_hi": 4, "z_lo": 2, "x_hi": 2, "x_lo": 2, "y_hi": 2, "core": 2}
F32 = jnp.float32
BF = jnp.bfloat16
VMEM_MAIN = 56
PANELS = 11


def mm(a, b):
    return lax.dot_general(a, b, (((1,), (0,)), ((), ())), preferred_element_type=F32)


def mm_nt(a, b):
    return lax.dot_general(a, b, (((1,), (1,)), ((), ())), preferred_element_type=F32)


def mm_tn(a, b):
    return lax.dot_general(a, b, (((0,), (0,)), ((), ())), preferred_element_type=F32)


def split(value):
    high = value.astype(BF)
    return high, (value - high.astype(F32)).astype(BF)


def halves(ref, value):
    width = value.shape[1] // 2
    ref[0] = value[:, :width].astype(ref.dtype)
    ref[1] = value[:, width:].astype(ref.dtype)


def main_kernel(
    core_ref,
    place_ref,
    pair_hbm,
    other_hbm,
    mate_hbm,
    opposite_hbm,
    mesh_hbm,
    w_em_hbm,
    g_hbm,
    w_eg_hbm,
    w_e2_hbm,
    w_node_hbm,
    cot_hbm,
    w_out_hbm,
    b_edge_hbm,
    b_node_hbm,
    slot_ref,
    pair_out,
    other_out,
    mate_out,
    opposite_out,
    grid_hbm,
    send_hbm,
    keep_hbm,
    pair_ref,
    other_ref,
    mate_ref,
    opposite_ref,
    mesh_ref,
    w_em_ref,
    g_ref,
    w_eg_ref,
    w_e2_ref,
    w_node_ref,
    cot_ref,
    w_out_ref,
    b_edge_ref,
    b_node_ref,
    grid_ref,
    send_ref,
    keep_ref,
    sems,
    out_sems,
    ext_ref,
    ng_half,
    og_half,
    ag_half,
    es_half,
    sl_half,
    slope_ref,
    og_ref,
    wo_ref,
):
    ways = (
        (mesh_hbm, mesh_ref),
        (pair_hbm, pair_ref),
        (other_hbm, other_ref),
        (mate_hbm, mate_ref),
        (opposite_hbm, opposite_ref),
        (w_em_hbm, w_em_ref),
        (g_hbm, g_ref),
        (w_eg_hbm, w_eg_ref),
        (b_edge_hbm, b_edge_ref),
        (b_node_hbm, b_node_ref),
        (w_e2_hbm, w_e2_ref),
        (w_node_hbm, w_node_ref),
        (cot_hbm, cot_ref),
        (w_out_hbm, w_out_ref),
    )
    copies = [pltpu.make_async_copy(a, b, sems.at[i]) for i, (a, b) in enumerate(ways)]
    for copy in copies:
        copy.start()
    core = core_ref[0]
    points = 256
    ext_ref[64:, :] = jnp.zeros((64, D), F32)
    for copy in copies[:5]:
        copy.wait()
    ext_ref[:64, :] = mesh_ref[...].astype(F32)
    ext_ref[64:82, :] = pair_ref[...].astype(F32)
    ext_ref[88:106, :] = other_ref[...].astype(F32)
    ext_ref[112:116, :] = mate_ref[...].astype(F32)
    ext_ref[120:124, :] = opposite_ref[...].astype(F32)
    ext = ext_ref[...].astype(BF)
    row = lax.broadcasted_iota(jnp.int32, (128, points), 0)
    hots = [jnp.where(row == (place_ref[k : k + 1, :] & 1023), 1.0, 0.0).astype(BF) for k in range(3)]
    copies[5].wait()
    projected = mm(ext, w_em_ref[...])
    high, low = split(projected)
    both = jnp.concatenate([high, low], axis=0)
    copies[6].wait()
    for copy in copies[7:10]:
        copy.wait()
    g = g_ref[...]
    grid_proj = mm(g, w_eg_ref[...]) + b_edge_ref[...]
    hidden_sum = None
    for k in range(3):
        pre = mm_tn(jnp.concatenate([hots[k], hots[k]], axis=0), both) + grid_proj
        sigma = jax.nn.sigmoid(pre)
        hidden = (pre * sigma).astype(BF)
        slope_ref[k] = sigma * (1.0 + pre * (1.0 - sigma))
        hidden = hidden.astype(F32)
        hidden_sum = hidden if hidden_sum is None else hidden_sum + hidden
    hs_high, hs_low = split(hidden_sum)
    for copy in copies[10:]:
        copy.wait()
    og_ref[...] = jnp.zeros_like(og_ref)
    wo_ref[...] = jnp.zeros_like(wo_ref)
    cot = cot_ref[...]
    og_ref[:CH, :] = jnp.where(place_ref[0:1, :] < 1024, cot, jnp.zeros_like(cot))
    wo_ref[:CH, :] = w_out_ref[...]
    out_grad = og_ref[...].T
    halves(og_half, out_grad)

    aggregate = (mm(hs_high, w_e2_ref[...]) + mm(hs_low, w_e2_ref[...])).astype(BF)
    node_pre = mm(g, w_node_ref[:D, :]) + mm(aggregate, w_node_ref[D:, :]) + b_node_ref[...]
    sigma = jax.nn.sigmoid(node_pre)
    node_hidden = (node_pre * sigma).astype(BF)
    node_grad = (mm(out_grad, wo_ref[...]) * (sigma * (1.0 + node_pre * (1.0 - sigma)))).astype(BF)
    halves(ng_half, node_grad)
    agg_grad = mm_nt(node_grad, w_node_ref[D:, :]).astype(BF)
    halves(ag_half, agg_grad)
    hidden_grad = mm_nt(agg_grad, w_e2_ref[...])
    edge_sum = None
    slots = None
    for k in range(3):
        edge_grad = (hidden_grad * slope_ref[k]).astype(BF)
        part = mm(hots[k], edge_grad)
        slots = part if slots is None else slots + part
        edge_grad = edge_grad.astype(F32)
        edge_sum = edge_grad if edge_sum is None else edge_sum + edge_grad
    edge_sum = edge_sum.astype(BF)
    halves(es_half, edge_sum)
    slot_ref[...] = slots[:64]
    pair_out[...] = slots[64:82].astype(BF)
    other_out[...] = slots[88:106].astype(BF)
    mate_out[...] = slots[112:116]
    opposite_out[...] = slots[120:124]
    sl_high, sl_low = split(slots)
    halves(sl_half, jnp.concatenate([sl_high, sl_low], axis=0))
    grid_ref[...] = mm_nt(node_grad, w_node_ref[:D, :]) + mm_nt(edge_sum, w_eg_ref[...])

    grid_copy = pltpu.make_async_copy(grid_ref, grid_hbm, out_sems.at[0])
    grid_copy.start()

    def put(ref, panel, value):
        v = value.reshape(2, 4, 2, 4, 8, 128)
        for i in range(16):
            tile = v[i >> 3, :, (i >> 2) & 1, i & 3]
            ref[i, panel * 32 : panel * 32 + 32, :] = tile.reshape(32, 128).astype(BF)

    def put_wide(ref, panel, value):
        put(ref, panel, value[:, :128])
        put(ref, panel + 1, value[:, 128:])

    ext_both = jnp.concatenate([ext, ext], axis=0)
    out_copies = [grid_copy]
    for ref, out, which in ((send_ref, send_hbm, 1 - core), (keep_ref, keep_hbm, core)):
        put_wide(ref, 0, mm_tn(ext_both, sl_half[which]))
        put_wide(ref, 2, mm_tn(g, es_half[which]))
        ag = ag_half[which]
        put_wide(ref, 4, mm_tn(hs_high, ag) + mm_tn(hs_low, ag))
        ng = ng_half[which]
        for half, left in enumerate((g, aggregate)):
            v = mm_tn(left, ng).reshape(4, 2, 4, 2, 8, 256)
            for i in range(8):
                for eight in range(2):
                    tile = v[:, i >> 2, i & 3, eight].reshape(32, 256).astype(BF)
                    for wide in range(2):
                        at = (6 + 2 * eight + wide) * 32
                        ref[8 * half + i, at : at + 32, :] = tile[:, wide * 128 : wide * 128 + 128]
        put(ref, 10, mm_tn(node_hidden, og_half[which]))
        copy = pltpu.make_async_copy(ref, out, out_sems.at[len(out_copies)])
        copy.start()
        out_copies.append(copy)
    for copy in out_copies:
        copy.wait()


def vmem(n):
    return [pl.BlockSpec(memory_space=pltpu.VMEM)] * n


def smem(n):
    return [pl.BlockSpec(memory_space=pltpu.SMEM)] * n


def params(mebibytes):
    return pltpu.CompilerParams(vmem_limit_bytes=mebibytes * 1024 * 1024)


ROWS = PANELS * 32


def main_call(*args):
    shape = jax.ShapeDtypeStruct
    inputs = args[2:]
    hbm = pl.BlockSpec(memory_space=pltpu.HBM)
    return pl.pallas_call(
        main_kernel,
        out_shape=(
            shape((64, D), F32),
            shape((18, D), BF),
            shape((18, D), BF),
            shape((4, D), F32),
            shape((4, D), F32),
            shape((256, D), F32),
            shape((16, ROWS, 128), BF),
            shape((16, ROWS, 128), BF),
        ),
        in_specs=smem(1) + vmem(1) + [hbm] * len(inputs),
        out_specs=tuple(vmem(5) + [hbm] * 3),
        scratch_shapes=[pltpu.VMEM(a.shape, a.dtype) for a in inputs]
        + [
            pltpu.VMEM((256, D), F32),
            pltpu.VMEM((16, ROWS, 128), BF),
            pltpu.VMEM((16, ROWS, 128), BF),
            pltpu.SemaphoreType.DMA((len(inputs),)),
            pltpu.SemaphoreType.DMA((3,)),
            pltpu.VMEM((128, D), F32),
            pltpu.VMEM((2, 256, 256), BF),
            pltpu.VMEM((2, 256, 128), BF),
            pltpu.VMEM((2, 256, 256), BF),
            pltpu.VMEM((2, 256, 256), BF),
            pltpu.VMEM((2, 256, 256), BF),
            pltpu.VMEM((3, 256, D), F32),
            pltpu.VMEM((256, 256), BF),
            pltpu.VMEM((256, D), BF),
        ],
        compiler_params=params(VMEM_MAIN),
        name="decoder_grads",
    )(*args)


def near_sum_kernel(in_ref, out_ref):
    total = in_ref[0].astype(F32)
    for i in range(1, 16):
        total = total + in_ref[i].astype(F32)
    total = total.reshape(PANELS, 4, 8, 128)
    for i in range(4):
        out_ref[i] = total[:, i].reshape(PANELS * 8, 128).astype(BF)


def near_sum(chunks):
    return pl.pallas_call(
        near_sum_kernel,
        out_shape=jax.ShapeDtypeStruct((4, PANELS * 8, 128), BF),
        in_specs=vmem(1),
        out_specs=vmem(1)[0],
        compiler_params=params(6),
        name="sum_over_near",
    )(chunks)


def far_sum_kernel(in_ref, out_ref):
    out_ref[...] = jnp.sum(in_ref[...].astype(F32), axis=0).astype(BF)


def far_sum(chunks):
    return pl.pallas_call(
        far_sum_kernel,
        out_shape=jax.ShapeDtypeStruct((PANELS * 8, 128), BF),
        in_specs=vmem(1),
        out_specs=vmem(1)[0],
        compiler_params=params(4),
        name="sum_over_far",
    )(chunks)


def last_kernel(in_ref, em_ref, eg_ref, e2_ref, node_ref, out_ref):
    for core in range(2):
        total = in_ref[core].astype(F32) + in_ref[core + 2].astype(F32)

        def panel(i):
            return total[8 * i : 8 * i + 8, :]

        for wide in range(2):
            at = slice((2 * core + wide) * 128, (2 * core + wide) * 128 + 128)
            em_ref[:, at] = panel(wide)
            eg_ref[:, at] = panel(2 + wide)
            e2_ref[:, at] = panel(4 + wide)
            node_ref[:8, at] = panel(6 + wide)
            node_ref[8:, at] = panel(8 + wide)
        if core == 0:
            out_ref[:, :128] = panel(10)
        else:
            out_ref[:, 128:] = panel(10)[:, : CH - 128]


def last(gathered):
    shape = jax.ShapeDtypeStruct
    return pl.pallas_call(
        last_kernel,
        out_shape=(
            shape((8, D), F32),
            shape((8, D), F32),
            shape((8, D), F32),
            shape((16, D), F32),
            shape((8, CH), F32),
        ),
        in_specs=vmem(1),
        out_specs=tuple(vmem(5)),
        compiler_params=params(4),
        name="sum_over_lon",
    )(gathered)


def to_pair(value):
    return lax.ppermute(value, "x_lo", [(0, 1), (1, 0)])


def to_other(value):
    odd = [(i, i + 1) for i in range(1, 63, 2)]
    return lax.ppermute(value, LAT, odd + [(j, i) for i, j in odd])


def to_mate(value):
    return lax.ppermute(value, "core", [(0, 1), (1, 0)])


def to_opposite(value):
    return lax.ppermute(value, LON, [(i, 3 - i) for i in range(4)])


def on_device(
    grid_latent,
    mesh_latent,
    cotangent,
    neighbours,
    live,
    w_em,
    w_eg,
    w_e2,
    w_node,
    w_out,
    bias_edge,
    bias_node,
):
    core = lax.axis_index("core").astype(jnp.int32)
    odd = lax.axis_index("x_lo").astype(jnp.int32)
    first, final = mesh_latent[:, 0], mesh_latent[:, 15]
    mate = to_mate(jnp.where(core == 0, final, first))
    opposite = to_opposite(jnp.where(core == 0, first, final))
    west = jnp.where(core == 0, opposite, mate)
    east = jnp.where(core == 0, mate, opposite)
    top = jnp.concatenate([west[:1], mesh_latent[0], east[:1]], axis=0)
    bottom = jnp.concatenate([west[3:], mesh_latent[3], east[3:]], axis=0)
    pair, other = jnp.where(odd == 1, top, bottom), jnp.where(odd == 1, bottom, top)
    slot = neighbours[0, 0]
    r, c = slot // 18, slot % 18
    side = jnp.where(c == 0, 120 - 8 * core, 112 + 8 * core) + r - 1
    inner = jnp.where((c == 0) | (c == 17), side, (r - 1) * 16 + c - 1)
    place = jnp.where(r == 0, 88 - 24 * odd + c, jnp.where(r == 5, 64 + 24 * odd + c, inner))
    place = jnp.where(lax.broadcasted_iota(jnp.int32, (3, 256), 1) < live[0, 0], place, place + 1024)
    pair, other, place = lax.optimization_barrier((pair, other, place))
    pair = to_pair(pair)
    other = to_other(other)
    slots, pair, other, mate, opposite, grid_grad, send, keep = main_call(
        core.reshape(1),
        place,
        pair,
        other,
        mate,
        opposite,
        mesh_latent.reshape(64, D),
        w_em,
        grid_latent[0, 0],
        w_eg,
        w_e2,
        w_node,
        cotangent[0, 0].T,
        w_out.T,
        bias_edge.reshape(1, D),
        bias_node.reshape(1, D),
    )
    got = to_mate(send)
    chunks = (keep.astype(F32) + got.astype(F32)).astype(BF)
    chunks, pair, other = lax.optimization_barrier((chunks, pair, other))
    chunks = lax.all_to_all(chunks, NEAR, 0, 0, tiled=True)
    chunks = lax.all_to_all(near_sum(chunks), "z_hi", 0, 0, tiled=True)
    part = far_sum(chunks)
    gathered = lax.all_gather(part, LON, axis=0, tiled=False)
    grads = last(gathered)

    pair = to_pair(pair).astype(F32)
    other = to_other(other).astype(F32)
    top = jnp.where(odd == 1, pair, other)
    bottom = jnp.where(odd == 1, other, pair)
    ends = jnp.stack([top, jnp.zeros_like(top), jnp.zeros_like(top), bottom])
    mate = mate + jnp.where(core == 0, ends[:, 17], ends[:, 0])
    opposite = opposite + jnp.where(core == 0, ends[:, 0], ends[:, 17])
    mate = to_mate(mate.astype(BF)).astype(F32)
    opposite = to_opposite(opposite.astype(BF)).astype(F32)
    west = jnp.where(core == 0, opposite, mate)
    east = jnp.where(core == 0, mate, opposite)
    sides = jnp.concatenate([west[:, None], jnp.zeros((4, 14, D), F32), east[:, None]], axis=1)
    owned = slots.reshape(4, 16, D) + ends[:, 1:17] + sides
    node_sum = owned.reshape(64, D).astype(BF)
    mesh_grad = mm_nt(node_sum, w_em).reshape(4, 16, D)
    return (grid_grad.reshape(1, 1, 256, D), mesh_grad) + tuple(grads)


def solution(mesh):
    fine = Mesh(mesh.devices.reshape(tuple(SIZES.values())), tuple(SIZES))
    in_specs = (
        P(LAT, LON, None, None),
        P(LAT, LON, None),
        P(LAT, LON, None, None),
        P(LAT, LON, None, None),
        P(LAT, LON),
    ) + (P(),) * 7
    out_specs = (P(LAT, LON, None, None), P(LAT, LON, None)) + (P(LAT, None),) * 5
    return jax.shard_map(
        on_device, mesh=fine, in_specs=in_specs, out_specs=out_specs, check_vma=False
    )
```

```python
import jax
import jax.numpy as jnp
from jax import lax
from jax.experimental import pallas as pl
from jax.experimental.pallas import tpu as pltpu
from jax.sharding import Mesh
from jax.sharding import PartitionSpec as P

D = 512
CH = 227
LAT = ("y_lo", "z_hi", "z_lo", "x_hi", "x_lo")
LON = ("y_hi", "core")
NEAR = ("y_lo", "z_lo", "x_hi", "x_lo")
FAR = ("z_hi", "y_hi")
SIZES = {"y_lo": 2, "z_hi": 4, "z_lo": 2, "x_hi": 2, "x_lo": 2, "y_hi": 2, "core": 2}
F32 = jnp.float32
BF = jnp.bfloat16
VMEM_MAIN = 56
PANELS = 11


def mm(a, b):
    return lax.dot_general(a, b, (((1,), (0,)), ((), ())), preferred_element_type=F32)


def mm_nt(a, b):
    return lax.dot_general(a, b, (((1,), (1,)), ((), ())), preferred_element_type=F32)


def mm_tn(a, b):
    return lax.dot_general(a, b, (((0,), (0,)), ((), ())), preferred_element_type=F32)


def split(value):
    high = value.astype(BF)
    return high, (value - high.astype(F32)).astype(BF)


def halves(ref, value):
    width = value.shape[1] // 2
    ref[0] = value[:, :width].astype(ref.dtype)
    ref[1] = value[:, width:].astype(ref.dtype)


def main_kernel(
    core_ref,
    odd_ref,
    live_ref,
    nbr_hbm,
    pair_hbm,
    other_hbm,
    mate_hbm,
    opposite_hbm,
    mesh_hbm,
    w_em_hbm,
    g_hbm,
    w_eg_hbm,
    w_e2_hbm,
    w_node_hbm,
    cot_hbm,
    w_out_hbm,
    b_edge_hbm,
    b_node_hbm,
    slot_ref,
    pair_out,
    other_out,
    mate_out,
    opposite_out,
    grid_hbm,
    send_hbm,
    keep_hbm,
    nbr_ref,
    pair_ref,
    other_ref,
    mate_ref,
    opposite_ref,
    mesh_ref,
    w_em_ref,
    g_ref,
    w_eg_ref,
    w_e2_ref,
    w_node_ref,
    cot_ref,
    w_out_ref,
    b_edge_ref,
    b_node_ref,
    grid_ref,
    send_ref,
    keep_ref,
    sems,
    out_sems,
    ext_ref,
    ng_half,
    og_half,
    ag_half,
    es_half,
    sl_half,
    slope_ref,
    og_ref,
    wo_ref,
):
    ways = (
        (nbr_hbm, nbr_ref),
        (mesh_hbm, mesh_ref),
        (pair_hbm, pair_ref),
        (other_hbm, other_ref),
        (mate_hbm, mate_ref),
        (opposite_hbm, opposite_ref),
        (w_em_hbm, w_em_ref),
        (g_hbm, g_ref),
        (w_eg_hbm, w_eg_ref),
        (b_edge_hbm, b_edge_ref),
        (w_e2_hbm, w_e2_ref),
        (w_node_hbm, w_node_ref),
        (cot_hbm, cot_ref),
        (w_out_hbm, w_out_ref),
        (b_node_hbm, b_node_ref),
    )
    copies = [pltpu.make_async_copy(a, b, sems.at[i]) for i, (a, b) in enumerate(ways)]
    for copy in copies[:10]:
        copy.start()
    core = core_ref[0]
    odd = odd_ref[0]
    points = 256
    ext_ref[64:, :] = jnp.zeros((64, D), F32)
    for copy in copies[:6]:
        copy.wait()
    ext_ref[:64, :] = mesh_ref[...].astype(F32)
    ext_ref[64:82, :] = pair_ref[...].astype(F32)
    ext_ref[88:106, :] = other_ref[...].astype(F32)
    ext_ref[112:116, :] = mate_ref[...].astype(F32)
    ext_ref[120:124, :] = opposite_ref[...].astype(F32)
    ext = ext_ref[...].astype(BF)
    row = lax.broadcasted_iota(jnp.int32, (128, points), 0)
    hots = []
    for k in range(3):
        slot = nbr_ref[k]
        r = (slot * 3641) >> 16
        c = slot - r * 18
        side = jnp.where(c == 0, 119 - 8 * core, 111 + 8 * core) + r
        inner = jnp.where((c == 0) | (c == 17), side, (r - 1) * 16 + c - 1)
        place = jnp.where(r == 0, 88 - 24 * odd + c, jnp.where(r == 5, 64 + 24 * odd + c, inner))
        hots.append(jnp.where(row == place, 1.0, 0.0).astype(BF))
    copies[6].wait()
    for copy in copies[10:]:
        copy.start()
    projected = mm(ext, w_em_ref[...])
    high, low = split(projected)
    both = jnp.concatenate([high, low], axis=0)
    for copy in copies[7:10]:
        copy.wait()
    g = g_ref[...]
    grid_proj = mm(g, w_eg_ref[...]) + b_edge_ref[...]
    hidden_sum = None
    for k in range(3):
        pre = mm_tn(jnp.concatenate([hots[k], hots[k]], axis=0), both) + grid_proj
        sigma = jax.nn.sigmoid(pre)
        hidden = (pre * sigma).astype(BF)
        slope_ref[k] = sigma * (1.0 + pre * (1.0 - sigma))
        hidden = hidden.astype(F32)
        hidden_sum = hidden if hidden_sum is None else hidden_sum + hidden
    hs_high, hs_low = split(hidden_sum)
    for copy in copies[10:]:
        copy.wait()
    og_ref[...] = jnp.zeros_like(og_ref)
    wo_ref[...] = jnp.zeros_like(wo_ref)
    column = lax.broadcasted_iota(jnp.int32, (CH, points), 1)
    cot = cot_ref[...]
    og_ref[:CH, :] = jnp.where(column < live_ref[0], cot, jnp.zeros_like(cot))
    wo_ref[:CH, :] = w_out_ref[...]
    out_grad = og_ref[...].T
    halves(og_half, out_grad)

    aggregate = (mm(hs_high, w_e2_ref[...]) + mm(hs_low, w_e2_ref[...])).astype(BF)
    node_pre = mm(g, w_node_ref[:D, :]) + mm(aggregate, w_node_ref[D:, :]) + b_node_ref[...]
    sigma = jax.nn.sigmoid(node_pre)
    node_hidden = (node_pre * sigma).astype(BF)
    node_grad = (mm(out_grad, wo_ref[...]) * (sigma * (1.0 + node_pre * (1.0 - sigma)))).astype(BF)
    halves(ng_half, node_grad)
    agg_grad = mm_nt(node_grad, w_node_ref[D:, :]).astype(BF)
    halves(ag_half, agg_grad)
    hidden_grad = mm_nt(agg_grad, w_e2_ref[...])
    edge_sum = None
    slots = None
    for k in range(3):
        edge_grad = (hidden_grad * slope_ref[k]).astype(BF)
        part = mm(hots[k], edge_grad)
        slots = part if slots is None else slots + part
        edge_grad = edge_grad.astype(F32)
        edge_sum = edge_grad if edge_sum is None else edge_sum + edge_grad
    edge_sum = edge_sum.astype(BF)
    halves(es_half, edge_sum)
    slot_ref[...] = slots[:64]
    pair_out[...] = slots[64:82].astype(BF)
    other_out[...] = slots[88:106].astype(BF)
    mate_out[...] = slots[112:116]
    opposite_out[...] = slots[120:124]
    sl_high, sl_low = split(slots)
    halves(sl_half, jnp.concatenate([sl_high, sl_low], axis=0))
    grid_ref[...] = mm_nt(node_grad, w_node_ref[:D, :]) + mm_nt(edge_sum, w_eg_ref[...])

    grid_copy = pltpu.make_async_copy(grid_ref, grid_hbm, out_sems.at[0])
    grid_copy.start()

    def put(ref, panel, value):
        v = value.reshape(2, 4, 2, 4, 8, 128)
        for i in range(16):
            tile = v[i >> 3, :, (i >> 2) & 1, i & 3]
            ref[i, panel * 32 : panel * 32 + 32, :] = tile.reshape(32, 128).astype(BF)

    def put_wide(ref, panel, value):
        put(ref, panel, value[:, :128])
        put(ref, panel + 1, value[:, 128:])

    ext_both = jnp.concatenate([ext, ext], axis=0)
    out_copies = [grid_copy]

    def leave(ref, out, first, end):
        rows = slice(first * 32, end * 32)
        copy = pltpu.make_async_copy(ref.at[:, rows], out.at[:, rows], out_sems.at[len(out_copies)])
        copy.start()
        out_copies.append(copy)

    for ref, out, which in ((send_ref, send_hbm, 1 - core), (keep_ref, keep_hbm, core)):
        put_wide(ref, 0, mm_tn(ext_both, sl_half[which]))
        put_wide(ref, 2, mm_tn(g, es_half[which]))
        ag = ag_half[which]
        put_wide(ref, 4, mm_tn(hs_high, ag) + mm_tn(hs_low, ag))
        leave(ref, out, 0, 6)
        ng = ng_half[which]
        for half, left in enumerate((g, aggregate)):
            v = mm_tn(left, ng).reshape(4, 2, 4, 2, 8, 256)
            for i in range(8):
                for eight in range(2):
                    tile = v[:, i >> 2, i & 3, eight].reshape(32, 256).astype(BF)
                    for wide in range(2):
                        at = (6 + 2 * eight + wide) * 32
                        ref[8 * half + i, at : at + 32, :] = tile[:, wide * 128 : wide * 128 + 128]
        leave(ref, out, 6, 10)
        put(ref, 10, mm_tn(node_hidden, og_half[which]))
        leave(ref, out, 10, 11)
    for copy in out_copies:
        copy.wait()


def vmem(n):
    return [pl.BlockSpec(memory_space=pltpu.VMEM)] * n


def smem(n):
    return [pl.BlockSpec(memory_space=pltpu.SMEM)] * n


def params(mebibytes):
    return pltpu.CompilerParams(vmem_limit_bytes=mebibytes * 1024 * 1024)


ROWS = PANELS * 32


def main_call(*args):
    shape = jax.ShapeDtypeStruct
    inputs = args[3:]
    hbm = pl.BlockSpec(memory_space=pltpu.HBM)
    return pl.pallas_call(
        main_kernel,
        out_shape=(
            shape((64, D), F32),
            shape((18, D), BF),
            shape((18, D), BF),
            shape((4, D), F32),
            shape((4, D), F32),
            shape((256, D), F32),
            shape((16, ROWS, 128), BF),
            shape((16, ROWS, 128), BF),
        ),
        in_specs=smem(3) + [hbm] * len(inputs),
        out_specs=tuple(vmem(5) + [hbm] * 3),
        scratch_shapes=[pltpu.VMEM(a.shape, a.dtype) for a in inputs]
        + [
            pltpu.VMEM((256, D), F32),
            pltpu.VMEM((16, ROWS, 128), BF),
            pltpu.VMEM((16, ROWS, 128), BF),
            pltpu.SemaphoreType.DMA((len(inputs),)),
            pltpu.SemaphoreType.DMA((7,)),
            pltpu.VMEM((128, D), F32),
            pltpu.VMEM((2, 256, 256), BF),
            pltpu.VMEM((2, 256, 128), BF),
            pltpu.VMEM((2, 256, 256), BF),
            pltpu.VMEM((2, 256, 256), BF),
            pltpu.VMEM((2, 256, 256), BF),
            pltpu.VMEM((3, 256, D), F32),
            pltpu.VMEM((256, 256), BF),
            pltpu.VMEM((256, D), BF),
        ],
        compiler_params=params(VMEM_MAIN),
        name="decoder_grads",
    )(*args)


def near_sum_kernel(in_ref, out_ref):
    total = in_ref[0].astype(F32)
    for i in range(1, 16):
        total = total + in_ref[i].astype(F32)
    total = total.reshape(PANELS, 4, 8, 128)
    for i in range(4):
        chunk = total[:, i].reshape(PANELS * 8, 128).astype(BF)
        out_ref[2 * i] = chunk
        out_ref[2 * i + 1] = chunk


def near_sum(chunks):
    return pl.pallas_call(
        near_sum_kernel,
        out_shape=jax.ShapeDtypeStruct((8, PANELS * 8, 128), BF),
        in_specs=vmem(1),
        out_specs=vmem(1)[0],
        compiler_params=params(6),
        name="sum_over_near",
    )(chunks)


def far_sum_kernel(in_ref, out_ref):
    out_ref[...] = jnp.sum(in_ref[...].astype(F32), axis=0).astype(BF)


def far_sum(chunks):
    return pl.pallas_call(
        far_sum_kernel,
        out_shape=jax.ShapeDtypeStruct((PANELS * 8, 128), BF),
        in_specs=vmem(1),
        out_specs=vmem(1)[0],
        compiler_params=params(4),
        name="sum_over_far",
    )(chunks)


def last_kernel(in_ref, em_ref, eg_ref, e2_ref, node_ref, out_ref):
    for core in range(2):
        total = in_ref[core].astype(F32)

        def panel(i):
            return total[8 * i : 8 * i + 8, :]

        for wide in range(2):
            at = slice((2 * core + wide) * 128, (2 * core + wide) * 128 + 128)
            em_ref[:, at] = panel(wide)
            eg_ref[:, at] = panel(2 + wide)
            e2_ref[:, at] = panel(4 + wide)
            node_ref[:8, at] = panel(6 + wide)
            node_ref[8:, at] = panel(8 + wide)
        if core == 0:
            out_ref[:, :128] = panel(10)
        else:
            out_ref[:, 128:] = panel(10)[:, : CH - 128]


def last(gathered):
    shape = jax.ShapeDtypeStruct
    return pl.pallas_call(
        last_kernel,
        out_shape=(
            shape((8, D), F32),
            shape((8, D), F32),
            shape((8, D), F32),
            shape((16, D), F32),
            shape((8, CH), F32),
        ),
        in_specs=vmem(1),
        out_specs=tuple(vmem(5)),
        compiler_params=params(4),
        name="share_over_core",
    )(gathered)


def to_pair(value):
    return lax.ppermute(value, "x_lo", [(0, 1), (1, 0)])


def to_other(value):
    odd = [(i, i + 1) for i in range(1, 63, 2)]
    return lax.ppermute(value, LAT, odd + [(j, i) for i, j in odd])


def to_mate(value):
    return lax.ppermute(value, "core", [(0, 1), (1, 0)])


def to_opposite(value):
    return lax.ppermute(value, LON, [(i, 3 - i) for i in range(4)])


def on_device(
    grid_latent,
    mesh_latent,
    cotangent,
    neighbours,
    live,
    w_em,
    w_eg,
    w_e2,
    w_node,
    w_out,
    bias_edge,
    bias_node,
):
    core = lax.axis_index("core").astype(jnp.int32)
    odd = lax.axis_index("x_lo").astype(jnp.int32)
    first, final = mesh_latent[:, 0], mesh_latent[:, 15]
    mate = to_mate(jnp.where(core == 0, final, first))
    opposite = to_opposite(jnp.where(core == 0, first, final))
    west = jnp.where(core == 0, opposite, mate)
    east = jnp.where(core == 0, mate, opposite)
    top = jnp.concatenate([west[:1], mesh_latent[0], east[:1]], axis=0)
    bottom = jnp.concatenate([west[3:], mesh_latent[3], east[3:]], axis=0)
    pair, other = jnp.where(odd == 1, top, bottom), jnp.where(odd == 1, bottom, top)
    pair = to_pair(pair)
    other = to_other(other)
    slots, pair, other, mate, opposite, grid_grad, send, keep = main_call(
        core.reshape(1),
        odd.reshape(1),
        live.reshape(1),
        jnp.swapaxes(neighbours, 1, 2).reshape(3, 1, 256),
        pair,
        other,
        mate,
        opposite,
        mesh_latent.reshape(64, D),
        w_em,
        grid_latent[0, 0],
        w_eg,
        w_e2,
        w_node,
        cotangent[0, 0].T,
        w_out.T,
        bias_edge.reshape(1, D),
        bias_node.reshape(1, D),
    )
    got = to_mate(send)
    chunks = (keep.astype(F32) + got.astype(F32)).astype(BF)
    chunks, pair, other = lax.optimization_barrier((chunks, pair, other))
    chunks = lax.all_to_all(chunks, NEAR, 0, 0, tiled=True)
    pair = to_pair(pair).astype(F32)
    other = to_other(other).astype(F32)
    top = jnp.where(odd == 1, pair, other)
    bottom = jnp.where(odd == 1, other, pair)
    ends = jnp.stack([top, jnp.zeros_like(top), jnp.zeros_like(top), bottom])
    mate = mate + jnp.where(core == 0, ends[:, 17], ends[:, 0])
    opposite = opposite + jnp.where(core == 0, ends[:, 0], ends[:, 17])
    mate, opposite = mate.astype(BF), opposite.astype(BF)
    chunks, mate, opposite = lax.optimization_barrier((near_sum(chunks), mate, opposite))
    chunks = lax.all_to_all(chunks, FAR, 0, 0, tiled=True)
    grads = last(lax.all_gather(far_sum(chunks), "core", axis=0, tiled=False))
    mate = to_mate(mate).astype(F32)
    opposite = to_opposite(opposite).astype(F32)
    west = jnp.where(core == 0, opposite, mate)
    east = jnp.where(core == 0, mate, opposite)
    sides = jnp.concatenate([west[:, None], jnp.zeros((4, 14, D), F32), east[:, None]], axis=1)
    owned = slots.reshape(4, 16, D) + ends[:, 1:17] + sides
    node_sum = owned.reshape(64, D).astype(BF)
    mesh_grad = mm_nt(node_sum, w_em).reshape(4, 16, D)
    return (grid_grad.reshape(1, 1, 256, D), mesh_grad) + tuple(grads)


def solution(mesh):
    fine = Mesh(mesh.devices.reshape(tuple(SIZES.values())), tuple(SIZES))
    in_specs = (
        P(LAT, LON, None, None),
        P(LAT, LON, None),
        P(LAT, LON, None, None),
        P(LAT, LON, None, None),
        P(LAT, LON),
    ) + (P(),) * 7
    out_specs = (P(LAT, LON, None, None), P(LAT, LON, None)) + (P(LAT, None),) * 5
    return jax.shard_map(
        on_device, mesh=fine, in_specs=in_specs, out_specs=out_specs, check_vma=False
    )
```

```python
import jax
import jax.numpy as jnp
from jax import lax
from jax.experimental import pallas as pl
from jax.experimental.pallas import tpu as pltpu
from jax.sharding import Mesh
from jax.sharding import PartitionSpec as P

D = 512
CH = 227
LAT = ("y_lo", "z_hi", "z_lo", "x_hi", "x_lo")
LON = ("y_hi", "core")
NEAR = ("y_lo", "z_lo", "x_hi", "x_lo")
FAR = ("z_hi", "y_hi")
SIZES = {"y_lo": 2, "z_hi": 4, "z_lo": 2, "x_hi": 2, "x_lo": 2, "y_hi": 2, "core": 2}
F32 = jnp.float32
BF = jnp.bfloat16
VMEM_MAIN = 56
PANELS = 11


def mm(a, b):
    return lax.dot_general(a, b, (((1,), (0,)), ((), ())), preferred_element_type=F32)


def mm_nt(a, b):
    return lax.dot_general(a, b, (((1,), (1,)), ((), ())), preferred_element_type=F32)


def mm_tn(a, b):
    return lax.dot_general(a, b, (((0,), (0,)), ((), ())), preferred_element_type=F32)


def split(value):
    high = value.astype(BF)
    return high, (value - high.astype(F32)).astype(BF)


def halves(ref, value):
    width = value.shape[1] // 2
    ref[0] = value[:, :width].astype(ref.dtype)
    ref[1] = value[:, width:].astype(ref.dtype)


def main_kernel(
    core_ref,
    odd_ref,
    live_ref,
    nbr_hbm,
    pair_hbm,
    other_hbm,
    mate_hbm,
    opposite_hbm,
    mesh_hbm,
    w_em_hbm,
    g_hbm,
    w_eg_hbm,
    w_e2_hbm,
    w_node_hbm,
    cot_hbm,
    w_out_hbm,
    b_edge_hbm,
    b_node_hbm,
    slot_ref,
    pair_out,
    other_out,
    mate_out,
    opposite_out,
    grid_hbm,
    send_hbm,
    keep_hbm,
    nbr_ref,
    pair_ref,
    other_ref,
    mate_ref,
    opposite_ref,
    mesh_ref,
    w_em_ref,
    g_ref,
    w_eg_ref,
    w_e2_ref,
    w_node_ref,
    cot_ref,
    w_out_ref,
    b_edge_ref,
    b_node_ref,
    grid_ref,
    send_ref,
    keep_ref,
    sems,
    out_sems,
    ext_ref,
    ng_half,
    og_half,
    ag_half,
    es_half,
    sl_half,
    slope_ref,
    og_ref,
    wo_ref,
):
    ways = (
        (nbr_hbm, nbr_ref),
        (mesh_hbm, mesh_ref),
        (pair_hbm, pair_ref),
        (other_hbm, other_ref),
        (mate_hbm, mate_ref),
        (opposite_hbm, opposite_ref),
        (w_em_hbm, w_em_ref),
        (g_hbm, g_ref),
        (w_eg_hbm, w_eg_ref),
        (b_edge_hbm, b_edge_ref),
        (w_e2_hbm, w_e2_ref),
        (w_node_hbm, w_node_ref),
        (cot_hbm, cot_ref),
        (w_out_hbm, w_out_ref),
        (b_node_hbm, b_node_ref),
    )
    copies = [pltpu.make_async_copy(a, b, sems.at[i]) for i, (a, b) in enumerate(ways)]
    for copy in copies[:10]:
        copy.start()
    core = core_ref[0]
    odd = odd_ref[0]
    points = 256
    ext_ref[64:, :] = jnp.zeros((64, D), F32)
    for copy in copies[:6]:
        copy.wait()
    ext_ref[:64, :] = mesh_ref[...].astype(F32)
    ext_ref[64:82, :] = pair_ref[...].astype(F32)
    ext_ref[88:106, :] = other_ref[...].astype(F32)
    ext_ref[112:116, :] = mate_ref[...].astype(F32)
    ext_ref[120:124, :] = opposite_ref[...].astype(F32)
    ext = ext_ref[...].astype(BF)
    row = lax.broadcasted_iota(jnp.int32, (128, points), 0)
    hots = []
    for k in range(3):
        slot = nbr_ref[k]
        r = (slot * 3641) >> 16
        c = slot - r * 18
        side = jnp.where(c == 0, 119 - 8 * core, 111 + 8 * core) + r
        inner = jnp.where((c == 0) | (c == 17), side, (r - 1) * 16 + c - 1)
        place = jnp.where(r == 0, 88 - 24 * odd + c, jnp.where(r == 5, 64 + 24 * odd + c, inner))
        hots.append(jnp.where(row == place, 1.0, 0.0).astype(BF))
    copies[6].wait()
    for copy in copies[10:]:
        copy.start()
    projected = mm(ext, w_em_ref[...])
    high, low = split(projected)
    both = jnp.concatenate([high, low], axis=0)
    for copy in copies[7:10]:
        copy.wait()
    g = g_ref[...]
    grid_proj = mm(g, w_eg_ref[...]) + b_edge_ref[...]
    hidden_sum = None
    for k in range(3):
        pre = mm_tn(jnp.concatenate([hots[k], hots[k]], axis=0), both) + grid_proj
        sigma = jax.nn.sigmoid(pre)
        hidden = (pre * sigma).astype(BF)
        slope_ref[k] = sigma * (1.0 + pre * (1.0 - sigma))
        hidden = hidden.astype(F32)
        hidden_sum = hidden if hidden_sum is None else hidden_sum + hidden
    hs_high, hs_low = split(hidden_sum)
    for copy in copies[10:]:
        copy.wait()
    og_ref[...] = jnp.zeros_like(og_ref)
    wo_ref[...] = jnp.zeros_like(wo_ref)
    column = lax.broadcasted_iota(jnp.int32, (CH, points), 1)
    cot = cot_ref[...]
    og_ref[:CH, :] = jnp.where(column < live_ref[0], cot, jnp.zeros_like(cot))
    wo_ref[:CH, :] = w_out_ref[...]
    out_grad = og_ref[...].T
    halves(og_half, out_grad)

    aggregate = (mm(hs_high, w_e2_ref[...]) + mm(hs_low, w_e2_ref[...])).astype(BF)
    node_pre = mm(g, w_node_ref[:D, :]) + mm(aggregate, w_node_ref[D:, :]) + b_node_ref[...]
    sigma = jax.nn.sigmoid(node_pre)
    node_hidden = (node_pre * sigma).astype(BF)
    node_grad = (mm(out_grad, wo_ref[...]) * (sigma * (1.0 + node_pre * (1.0 - sigma)))).astype(BF)
    halves(ng_half, node_grad)
    agg_grad = mm_nt(node_grad, w_node_ref[D:, :]).astype(BF)
    halves(ag_half, agg_grad)
    hidden_grad = mm_nt(agg_grad, w_e2_ref[...])
    edge_sum = None
    slots = None
    for k in range(3):
        edge_grad = (hidden_grad * slope_ref[k]).astype(BF)
        part = mm(hots[k], edge_grad)
        slots = part if slots is None else slots + part
        edge_grad = edge_grad.astype(F32)
        edge_sum = edge_grad if edge_sum is None else edge_sum + edge_grad
    edge_sum = edge_sum.astype(BF)
    halves(es_half, edge_sum)
    slot_ref[...] = slots[:64]
    pair_out[...] = slots[65:81]
    other_out[...] = slots[89:105]
    at_mate = [slots[112:116]]
    at_opposite = [slots[120:124]]
    for west_end, east_end in ((slots[64:65], slots[81:82]), (slots[88:89], slots[105:106])):
        at_mate.append(jnp.where(core == 0, east_end, west_end))
        at_opposite.append(jnp.where(core == 0, west_end, east_end))
    mate_out[...] = jnp.concatenate(at_mate, axis=0).astype(BF)
    opposite_out[...] = jnp.concatenate(at_opposite, axis=0).astype(BF)
    sl_high, sl_low = split(slots)
    halves(sl_half, jnp.concatenate([sl_high, sl_low], axis=0))
    grid_ref[...] = mm_nt(node_grad, w_node_ref[:D, :]) + mm_nt(edge_sum, w_eg_ref[...])

    grid_copy = pltpu.make_async_copy(grid_ref, grid_hbm, out_sems.at[0])
    grid_copy.start()

    def put(ref, panel, value):
        v = value.reshape(2, 4, 2, 4, 8, 128)
        for i in range(16):
            tile = v[i >> 3, :, (i >> 2) & 1, i & 3]
            ref[i, panel * 32 : panel * 32 + 32, :] = tile.reshape(32, 128).astype(BF)

    def put_wide(ref, panel, value):
        put(ref, panel, value[:, :128])
        put(ref, panel + 1, value[:, 128:])

    ext_both = jnp.concatenate([ext, ext], axis=0)
    out_copies = [grid_copy]

    def leave(ref, out, first, end):
        rows = slice(first * 32, end * 32)
        copy = pltpu.make_async_copy(ref.at[:, rows], out.at[:, rows], out_sems.at[len(out_copies)])
        copy.start()
        out_copies.append(copy)

    for ref, out, which in ((send_ref, send_hbm, 1 - core), (keep_ref, keep_hbm, core)):
        put_wide(ref, 0, mm_tn(ext_both, sl_half[which]))
        put_wide(ref, 2, mm_tn(g, es_half[which]))
        ag = ag_half[which]
        put_wide(ref, 4, mm_tn(hs_high, ag) + mm_tn(hs_low, ag))
        leave(ref, out, 0, 6)
        ng = ng_half[which]
        for half, left in enumerate((g, aggregate)):
            v = mm_tn(left, ng).reshape(4, 2, 4, 2, 8, 256)
            for i in range(8):
                for eight in range(2):
                    tile = v[:, i >> 2, i & 3, eight].reshape(32, 256).astype(BF)
                    for wide in range(2):
                        at = (6 + 2 * eight + wide) * 32
                        ref[8 * half + i, at : at + 32, :] = tile[:, wide * 128 : wide * 128 + 128]
        leave(ref, out, 6, 10)
        put(ref, 10, mm_tn(node_hidden, og_half[which]))
        leave(ref, out, 10, 11)
    for copy in out_copies:
        copy.wait()


def vmem(n):
    return [pl.BlockSpec(memory_space=pltpu.VMEM)] * n


def smem(n):
    return [pl.BlockSpec(memory_space=pltpu.SMEM)] * n


def params(mebibytes):
    return pltpu.CompilerParams(vmem_limit_bytes=mebibytes * 1024 * 1024)


ROWS = PANELS * 32


def main_call(*args):
    shape = jax.ShapeDtypeStruct
    inputs = args[3:]
    hbm = pl.BlockSpec(memory_space=pltpu.HBM)
    return pl.pallas_call(
        main_kernel,
        out_shape=(
            shape((64, D), F32),
            shape((16, D), F32),
            shape((16, D), F32),
            shape((6, D), BF),
            shape((6, D), BF),
            shape((256, D), F32),
            shape((16, ROWS, 128), BF),
            shape((16, ROWS, 128), BF),
        ),
        in_specs=smem(3) + [hbm] * len(inputs),
        out_specs=tuple(vmem(5) + [hbm] * 3),
        scratch_shapes=[pltpu.VMEM(a.shape, a.dtype) for a in inputs]
        + [
            pltpu.VMEM((256, D), F32),
            pltpu.VMEM((16, ROWS, 128), BF),
            pltpu.VMEM((16, ROWS, 128), BF),
            pltpu.SemaphoreType.DMA((len(inputs),)),
            pltpu.SemaphoreType.DMA((7,)),
            pltpu.VMEM((128, D), F32),
            pltpu.VMEM((2, 256, 256), BF),
            pltpu.VMEM((2, 256, 128), BF),
            pltpu.VMEM((2, 256, 256), BF),
            pltpu.VMEM((2, 256, 256), BF),
            pltpu.VMEM((2, 256, 256), BF),
            pltpu.VMEM((3, 256, D), F32),
            pltpu.VMEM((256, 256), BF),
            pltpu.VMEM((256, D), BF),
        ],
        compiler_params=params(VMEM_MAIN),
        name="decoder_grads",
    )(*args)


def near_sum_kernel(in_ref, out_ref):
    total = in_ref[0].astype(F32)
    for i in range(1, 16):
        total = total + in_ref[i].astype(F32)
    total = total.reshape(PANELS, 4, 8, 128)
    for i in range(4):
        chunk = total[:, i].reshape(PANELS * 8, 128).astype(BF)
        out_ref[2 * i] = chunk
        out_ref[2 * i + 1] = chunk


def near_sum(chunks):
    return pl.pallas_call(
        near_sum_kernel,
        out_shape=jax.ShapeDtypeStruct((8, PANELS * 8, 128), BF),
        in_specs=vmem(1),
        out_specs=vmem(1)[0],
        compiler_params=params(6),
        name="sum_over_near",
    )(chunks)


def far_sum_kernel(in_ref, out_ref):
    out_ref[...] = jnp.sum(in_ref[...].astype(F32), axis=0).astype(BF)


def far_sum(chunks):
    return pl.pallas_call(
        far_sum_kernel,
        out_shape=jax.ShapeDtypeStruct((PANELS * 8, 128), BF),
        in_specs=vmem(1),
        out_specs=vmem(1)[0],
        compiler_params=params(4),
        name="sum_over_far",
    )(chunks)


def last_kernel(in_ref, em_ref, eg_ref, e2_ref, node_ref, out_ref):
    for core in range(2):
        total = in_ref[core].astype(F32)

        def panel(i):
            return total[8 * i : 8 * i + 8, :]

        for wide in range(2):
            at = slice((2 * core + wide) * 128, (2 * core + wide) * 128 + 128)
            em_ref[:, at] = panel(wide)
            eg_ref[:, at] = panel(2 + wide)
            e2_ref[:, at] = panel(4 + wide)
            node_ref[:8, at] = panel(6 + wide)
            node_ref[8:, at] = panel(8 + wide)
        if core == 0:
            out_ref[:, :128] = panel(10)
        else:
            out_ref[:, 128:] = panel(10)[:, : CH - 128]


def last(gathered):
    shape = jax.ShapeDtypeStruct
    return pl.pallas_call(
        last_kernel,
        out_shape=(
            shape((8, D), F32),
            shape((8, D), F32),
            shape((8, D), F32),
            shape((16, D), F32),
            shape((8, CH), F32),
        ),
        in_specs=vmem(1),
        out_specs=tuple(vmem(5)),
        compiler_params=params(4),
        name="share_over_core",
    )(gathered)


def to_pair(value):
    return lax.ppermute(value, "x_lo", [(0, 1), (1, 0)])


def to_other(value):
    odd = [(i, i + 1) for i in range(1, 63, 2)]
    return lax.ppermute(value, LAT, odd + [(j, i) for i, j in odd])


def to_mate(value):
    return lax.ppermute(value, "core", [(0, 1), (1, 0)])


def to_opposite(value):
    return lax.ppermute(value, LON, [(i, 3 - i) for i in range(4)])


def on_device(
    grid_latent,
    mesh_latent,
    cotangent,
    neighbours,
    live,
    w_em,
    w_eg,
    w_e2,
    w_node,
    w_out,
    bias_edge,
    bias_node,
):
    core = lax.axis_index("core").astype(jnp.int32)
    odd = lax.axis_index("x_lo").astype(jnp.int32)
    first, final = mesh_latent[:, 0], mesh_latent[:, 15]
    mate = to_mate(jnp.where(core == 0, final, first))
    opposite = to_opposite(jnp.where(core == 0, first, final))
    west = jnp.where(core == 0, opposite, mate)
    east = jnp.where(core == 0, mate, opposite)
    top = jnp.concatenate([west[:1], mesh_latent[0], east[:1]], axis=0)
    bottom = jnp.concatenate([west[3:], mesh_latent[3], east[3:]], axis=0)
    pair, other = jnp.where(odd == 1, top, bottom), jnp.where(odd == 1, bottom, top)
    pair = to_pair(pair)
    other = to_other(other)
    slots, pair, other, mate, opposite, grid_grad, send, keep = main_call(
        core.reshape(1),
        odd.reshape(1),
        live.reshape(1),
        jnp.swapaxes(neighbours, 1, 2).reshape(3, 1, 256),
        pair,
        other,
        mate,
        opposite,
        mesh_latent.reshape(64, D),
        w_em,
        grid_latent[0, 0],
        w_eg,
        w_e2,
        w_node,
        cotangent[0, 0].T,
        w_out.T,
        bias_edge.reshape(1, D),
        bias_node.reshape(1, D),
    )
    got = to_mate(send)
    chunks = (keep.astype(F32) + got.astype(F32)).astype(BF)
    chunks, mate, opposite = lax.optimization_barrier((chunks, mate, opposite))
    chunks = lax.all_to_all(chunks, NEAR, 0, 0, tiled=True)
    chunks = lax.all_to_all(near_sum(chunks), FAR, 0, 0, tiled=True)
    grads = last(lax.all_gather(far_sum(chunks), "core", axis=0, tiled=False))

    mate = to_mate(mate).astype(F32)
    opposite = to_opposite(opposite).astype(F32)
    west = jnp.where(core == 0, opposite, mate)
    east = jnp.where(core == 0, mate, opposite)
    sides = jnp.concatenate([west[:, None], jnp.zeros((6, 14, D), F32), east[:, None]], axis=1)
    pair = to_pair((pair + sides[4]).astype(BF)).astype(F32)
    other = to_other((other + sides[5]).astype(BF)).astype(F32)
    top = jnp.where(odd == 1, pair, other)
    bottom = jnp.where(odd == 1, other, pair)
    ends = jnp.stack([top, jnp.zeros_like(top), jnp.zeros_like(top), bottom])
    owned = slots.reshape(4, 16, D) + ends + sides[:4]
    node_sum = owned.reshape(64, D).astype(BF)
    mesh_grad = mm_nt(node_sum, w_em).reshape(4, 16, D)
    return (grid_grad.reshape(1, 1, 256, D), mesh_grad) + tuple(grads)


def solution(mesh):
    fine = Mesh(mesh.devices.reshape(tuple(SIZES.values())), tuple(SIZES))
    in_specs = (
        P(LAT, LON, None, None),
        P(LAT, LON, None),
        P(LAT, LON, None, None),
        P(LAT, LON, None, None),
        P(LAT, LON),
    ) + (P(),) * 7
    out_specs = (P(LAT, LON, None, None), P(LAT, LON, None)) + (P(LAT, None),) * 5
    return jax.shard_map(
        on_device, mesh=fine, in_specs=in_specs, out_specs=out_specs, check_vma=False
    )
```

```python
import jax
import jax.numpy as jnp
from jax import lax
from jax.experimental import pallas as pl
from jax.experimental.pallas import tpu as pltpu
from jax.sharding import Mesh
from jax.sharding import PartitionSpec as P

D = 512
CH = 227
LAT = ("y_lo", "z_hi", "z_lo", "x_hi", "x_lo")
LON = ("y_hi", "core")
NEAR = ("y_lo", "z_lo", "x_hi", "x_lo")
FAR = ("z_hi", "y_hi")
SIZES = {"y_lo": 2, "z_hi": 4, "z_lo": 2, "x_hi": 2, "x_lo": 2, "y_hi": 2, "core": 2}
F32 = jnp.float32
BF = jnp.bfloat16
VMEM_MAIN = 56
PANELS = 11


def mm(a, b):
    return lax.dot_general(a, b, (((1,), (0,)), ((), ())), preferred_element_type=F32)


def mm_nt(a, b):
    return lax.dot_general(a, b, (((1,), (1,)), ((), ())), preferred_element_type=F32)


def mm_tn(a, b):
    return lax.dot_general(a, b, (((0,), (0,)), ((), ())), preferred_element_type=F32)


def split(value):
    high = value.astype(BF)
    return high, (value - high.astype(F32)).astype(BF)


def halves(ref, value):
    width = value.shape[1] // 2
    ref[0] = value[:, :width].astype(ref.dtype)
    ref[1] = value[:, width:].astype(ref.dtype)


def main_kernel(
    core_ref,
    odd_ref,
    live_ref,
    nbr_hbm,
    pair_hbm,
    other_hbm,
    mate_hbm,
    opposite_hbm,
    mesh_hbm,
    w_em_hbm,
    g_hbm,
    w_eg_hbm,
    w_e2_hbm,
    w_node_hbm,
    cot_hbm,
    w_out_hbm,
    b_edge_hbm,
    b_node_hbm,
    slot_ref,
    pair_out,
    other_out,
    mate_out,
    opposite_out,
    grid_hbm,
    send_hbm,
    keep_hbm,
    nbr_ref,
    pair_ref,
    other_ref,
    mate_ref,
    opposite_ref,
    mesh_ref,
    w_em_ref,
    g_ref,
    w_eg_ref,
    w_e2_ref,
    w_node_ref,
    cot_ref,
    w_out_ref,
    b_edge_ref,
    b_node_ref,
    grid_ref,
    send_ref,
    keep_ref,
    sems,
    out_sems,
    ext_ref,
    ng_half,
    og_half,
    ag_half,
    es_half,
    sl_half,
    slope_ref,
    og_ref,
    wo_ref,
):
    ways = (
        (nbr_hbm, nbr_ref),
        (mesh_hbm, mesh_ref),
        (pair_hbm, pair_ref),
        (other_hbm, other_ref),
        (mate_hbm, mate_ref),
        (opposite_hbm, opposite_ref),
        (w_em_hbm, w_em_ref),
        (g_hbm, g_ref),
        (w_eg_hbm, w_eg_ref),
        (b_edge_hbm, b_edge_ref),
        (w_e2_hbm, w_e2_ref),
        (w_node_hbm, w_node_ref),
        (cot_hbm, cot_ref),
        (w_out_hbm, w_out_ref),
        (b_node_hbm, b_node_ref),
    )
    copies = [pltpu.make_async_copy(a, b, sems.at[i]) for i, (a, b) in enumerate(ways)]
    for copy in copies[:10]:
        copy.start()
    core = core_ref[0]
    odd = odd_ref[0]
    points = 256
    ext_ref[64:, :] = jnp.zeros((64, D), F32)
    for copy in copies[:6]:
        copy.wait()
    ext_ref[:64, :] = mesh_ref[...].astype(F32)
    ext_ref[64:82, :] = pair_ref[...].astype(F32)
    ext_ref[88:106, :] = other_ref[...].astype(F32)
    ext_ref[112:116, :] = mate_ref[...].astype(F32)
    ext_ref[120:124, :] = opposite_ref[...].astype(F32)
    ext = ext_ref[...].astype(BF)
    row = lax.broadcasted_iota(jnp.int32, (128, points), 0)
    hots = []
    for k in range(3):
        slot = nbr_ref[k]
        r = (slot * 3641) >> 16
        c = slot - r * 18
        side = jnp.where(c == 0, 119 - 8 * core, 111 + 8 * core) + r
        inner = jnp.where((c == 0) | (c == 17), side, (r - 1) * 16 + c - 1)
        place = jnp.where(r == 0, 88 - 24 * odd + c, jnp.where(r == 5, 64 + 24 * odd + c, inner))
        hots.append(jnp.where(row == place, 1.0, 0.0).astype(BF))
    copies[6].wait()
    for copy in copies[10:]:
        copy.start()
    projected = mm(ext, w_em_ref[...])
    high, low = split(projected)
    both = jnp.concatenate([high, low], axis=0)
    for copy in copies[7:10]:
        copy.wait()
    g = g_ref[...]
    grid_proj = mm(g, w_eg_ref[...]) + b_edge_ref[...]
    hidden_sum = None
    for k in range(3):
        pre = mm_tn(jnp.concatenate([hots[k], hots[k]], axis=0), both) + grid_proj
        sigma = jax.nn.sigmoid(pre)
        hidden = (pre * sigma).astype(BF)
        slope_ref[k] = sigma * (1.0 + pre * (1.0 - sigma))
        hidden = hidden.astype(F32)
        hidden_sum = hidden if hidden_sum is None else hidden_sum + hidden
    hs_high, hs_low = split(hidden_sum)
    for copy in copies[10:]:
        copy.wait()
    og_ref[...] = jnp.zeros_like(og_ref)
    wo_ref[...] = jnp.zeros_like(wo_ref)
    column = lax.broadcasted_iota(jnp.int32, (CH, points), 1)
    cot = cot_ref[...]
    og_ref[:CH, :] = jnp.where(column < live_ref[0], cot, jnp.zeros_like(cot))
    wo_ref[:CH, :] = w_out_ref[...]
    out_grad = og_ref[...].T
    halves(og_half, out_grad)

    aggregate = (mm(hs_high, w_e2_ref[...]) + mm(hs_low, w_e2_ref[...])).astype(BF)
    node_pre = mm(g, w_node_ref[:D, :]) + mm(aggregate, w_node_ref[D:, :]) + b_node_ref[...]
    sigma = jax.nn.sigmoid(node_pre)
    node_hidden = (node_pre * sigma).astype(BF)
    node_grad = (mm(out_grad, wo_ref[...]) * (sigma * (1.0 + node_pre * (1.0 - sigma)))).astype(BF)
    halves(ng_half, node_grad)
    agg_grad = mm_nt(node_grad, w_node_ref[D:, :]).astype(BF)
    halves(ag_half, agg_grad)
    hidden_grad = mm_nt(agg_grad, w_e2_ref[...])
    edge_sum = None
    slots = None
    for k in range(3):
        edge_grad = (hidden_grad * slope_ref[k]).astype(BF)
        part = mm(hots[k], edge_grad)
        slots = part if slots is None else slots + part
        edge_grad = edge_grad.astype(F32)
        edge_sum = edge_grad if edge_sum is None else edge_sum + edge_grad
    edge_sum = edge_sum.astype(BF)
    halves(es_half, edge_sum)
    slot_ref[...] = slots[:64]
    pair_out[...] = slots[65:81]
    other_out[...] = slots[89:105]
    at_mate = [slots[112:116]]
    at_opposite = [slots[120:124]]
    for west_end, east_end in ((slots[64:65], slots[81:82]), (slots[88:89], slots[105:106])):
        at_mate.append(jnp.where(core == 0, east_end, west_end))
        at_opposite.append(jnp.where(core == 0, west_end, east_end))
    mate_out[...] = jnp.concatenate(at_mate, axis=0).astype(BF)
    opposite_out[...] = jnp.concatenate(at_opposite, axis=0).astype(BF)
    sl_high, sl_low = split(slots)
    halves(sl_half, jnp.concatenate([sl_high, sl_low], axis=0))
    grid_ref[...] = mm_nt(node_grad, w_node_ref[:D, :]) + mm_nt(edge_sum, w_eg_ref[...])

    grid_copy = pltpu.make_async_copy(grid_ref, grid_hbm, out_sems.at[0])
    grid_copy.start()

    def put(ref, panel, value):
        v = value.reshape(2, 4, 2, 4, 8, 128)
        for i in range(16):
            tile = v[i >> 3, :, (i >> 2) & 1, i & 3]
            ref[i, panel * 32 : panel * 32 + 32, :] = tile.reshape(32, 128).astype(BF)

    def put_wide(ref, panel, value):
        put(ref, panel, value[:, :128])
        put(ref, panel + 1, value[:, 128:])

    ext_both = jnp.concatenate([ext, ext], axis=0)
    out_copies = [grid_copy]

    def leave(ref, out, first, end):
        rows = slice(first * 32, end * 32)
        copy = pltpu.make_async_copy(ref.at[:, rows], out.at[:, rows], out_sems.at[len(out_copies)])
        copy.start()
        out_copies.append(copy)

    for ref, out, which in ((send_ref, send_hbm, 1 - core), (keep_ref, keep_hbm, core)):
        put_wide(ref, 0, mm_tn(ext_both, sl_half[which]))
        put_wide(ref, 2, mm_tn(g, es_half[which]))
        ag = ag_half[which]
        put_wide(ref, 4, mm_tn(hs_high, ag) + mm_tn(hs_low, ag))
        leave(ref, out, 0, 6)
        ng = ng_half[which]
        for half, left in enumerate((g, aggregate)):
            v = mm_tn(left, ng).reshape(4, 2, 4, 2, 8, 256)
            for i in range(8):
                for eight in range(2):
                    tile = v[:, i >> 2, i & 3, eight].reshape(32, 256).astype(BF)
                    for wide in range(2):
                        at = (6 + 2 * eight + wide) * 32
                        ref[8 * half + i, at : at + 32, :] = tile[:, wide * 128 : wide * 128 + 128]
        leave(ref, out, 6, 10)
        put(ref, 10, mm_tn(node_hidden, og_half[which]))
        leave(ref, out, 10, 11)
    for copy in out_copies:
        copy.wait()


def vmem(n):
    return [pl.BlockSpec(memory_space=pltpu.VMEM)] * n


def smem(n):
    return [pl.BlockSpec(memory_space=pltpu.SMEM)] * n


def params(mebibytes):
    return pltpu.CompilerParams(vmem_limit_bytes=mebibytes * 1024 * 1024)


ROWS = PANELS * 32


def main_call(*args):
    shape = jax.ShapeDtypeStruct
    inputs = args[3:]
    hbm = pl.BlockSpec(memory_space=pltpu.HBM)
    return pl.pallas_call(
        main_kernel,
        out_shape=(
            shape((64, D), F32),
            shape((16, D), F32),
            shape((16, D), F32),
            shape((6, D), BF),
            shape((6, D), BF),
            shape((256, D), F32),
            shape((16, ROWS, 128), BF),
            shape((16, ROWS, 128), BF),
        ),
        in_specs=smem(3) + [hbm] * len(inputs),
        out_specs=tuple(vmem(5) + [hbm] * 3),
        scratch_shapes=[pltpu.VMEM(a.shape, a.dtype) for a in inputs]
        + [
            pltpu.VMEM((256, D), F32),
            pltpu.VMEM((16, ROWS, 128), BF),
            pltpu.VMEM((16, ROWS, 128), BF),
            pltpu.SemaphoreType.DMA((len(inputs),)),
            pltpu.SemaphoreType.DMA((7,)),
            pltpu.VMEM((128, D), F32),
            pltpu.VMEM((2, 256, 256), BF),
            pltpu.VMEM((2, 256, 128), BF),
            pltpu.VMEM((2, 256, 256), BF),
            pltpu.VMEM((2, 256, 256), BF),
            pltpu.VMEM((2, 256, 256), BF),
            pltpu.VMEM((3, 256, D), F32),
            pltpu.VMEM((256, 256), BF),
            pltpu.VMEM((256, D), BF),
        ],
        compiler_params=params(VMEM_MAIN),
        name="decoder_grads",
    )(*args)


def near_sum_kernel(in_ref, out_ref):
    total = in_ref[0].astype(F32)
    for i in range(1, 16):
        total = total + in_ref[i].astype(F32)
    total = total.reshape(PANELS, 4, 8, 128)
    for i in range(4):
        chunk = total[:, i].reshape(PANELS * 8, 128).astype(BF)
        out_ref[2 * i] = chunk
        out_ref[2 * i + 1] = chunk


def near_sum(chunks):
    return pl.pallas_call(
        near_sum_kernel,
        out_shape=jax.ShapeDtypeStruct((8, PANELS * 8, 128), BF),
        in_specs=vmem(1),
        out_specs=vmem(1)[0],
        compiler_params=params(6),
        name="sum_over_near",
    )(chunks)


def far_sum_kernel(in_ref, out_ref):
    out_ref[...] = jnp.sum(in_ref[...].astype(F32), axis=0).astype(BF)


def far_sum(chunks):
    return pl.pallas_call(
        far_sum_kernel,
        out_shape=jax.ShapeDtypeStruct((PANELS * 8, 128), BF),
        in_specs=vmem(1),
        out_specs=vmem(1)[0],
        compiler_params=params(4),
        name="sum_over_far",
    )(chunks)


def last_kernel(in_ref, em_ref, eg_ref, e2_ref, node_ref, out_ref):
    for core in range(2):
        total = in_ref[core].astype(F32)

        def panel(i):
            return total[8 * i : 8 * i + 8, :]

        for wide in range(2):
            at = slice((2 * core + wide) * 128, (2 * core + wide) * 128 + 128)
            em_ref[:, at] = panel(wide)
            eg_ref[:, at] = panel(2 + wide)
            e2_ref[:, at] = panel(4 + wide)
            node_ref[:8, at] = panel(6 + wide)
            node_ref[8:, at] = panel(8 + wide)
        if core == 0:
            out_ref[:, :128] = panel(10)
        else:
            out_ref[:, 128:] = panel(10)[:, : CH - 128]


def last(gathered):
    shape = jax.ShapeDtypeStruct
    return pl.pallas_call(
        last_kernel,
        out_shape=(
            shape((8, D), F32),
            shape((8, D), F32),
            shape((8, D), F32),
            shape((16, D), F32),
            shape((8, CH), F32),
        ),
        in_specs=vmem(1),
        out_specs=tuple(vmem(5)),
        compiler_params=params(4),
        name="share_over_core",
    )(gathered)


def to_pair(value):
    return lax.ppermute(value, "x_lo", [(0, 1), (1, 0)])


def to_other(value):
    odd = [(i, i + 1) for i in range(1, 63, 2)]
    return lax.ppermute(value, LAT, odd + [(j, i) for i, j in odd])


def to_mate(value):
    return lax.ppermute(value, "core", [(0, 1), (1, 0)])


def to_opposite(value):
    return lax.ppermute(value, LON, [(i, 3 - i) for i in range(4)])


def on_device(
    grid_latent,
    mesh_latent,
    cotangent,
    neighbours,
    live,
    w_em,
    w_eg,
    w_e2,
    w_node,
    w_out,
    bias_edge,
    bias_node,
):
    core = lax.axis_index("core").astype(jnp.int32)
    odd = lax.axis_index("x_lo").astype(jnp.int32)
    first, final = mesh_latent[:, 0], mesh_latent[:, 15]
    mate = to_mate(jnp.where(core == 0, final, first))
    opposite = to_opposite(jnp.where(core == 0, first, final))
    west = jnp.where(core == 0, opposite, mate)
    east = jnp.where(core == 0, mate, opposite)
    top = jnp.concatenate([west[:1], mesh_latent[0], east[:1]], axis=0)
    bottom = jnp.concatenate([west[3:], mesh_latent[3], east[3:]], axis=0)
    pair, other = jnp.where(odd == 1, top, bottom), jnp.where(odd == 1, bottom, top)
    pair = to_pair(pair)
    other = to_other(other)
    slots, pair, other, mate, opposite, grid_grad, send, keep = main_call(
        core.reshape(1),
        odd.reshape(1),
        live.reshape(1),
        jnp.swapaxes(neighbours, 1, 2).reshape(3, 1, 256),
        pair,
        other,
        mate,
        opposite,
        mesh_latent.reshape(64, D),
        w_em,
        grid_latent[0, 0],
        w_eg,
        w_e2,
        w_node,
        cotangent[0, 0].T,
        w_out.T,
        bias_edge.reshape(1, D),
        bias_node.reshape(1, D),
    )
    got = to_mate(send)
    chunks = (keep.astype(F32) + got.astype(F32)).astype(BF)
    mate = to_mate(mate).astype(F32)
    opposite = to_opposite(opposite).astype(F32)
    west = jnp.where(core == 0, opposite, mate)
    east = jnp.where(core == 0, mate, opposite)
    sides = jnp.concatenate([west[:, None], jnp.zeros((6, 14, D), F32), east[:, None]], axis=1)
    pair, other = (pair + sides[4]).astype(BF), (other + sides[5]).astype(BF)
    chunks, pair, other = lax.optimization_barrier((chunks, pair, other))
    chunks = lax.all_to_all(chunks, NEAR, 0, 0, tiled=True)
    chunks = lax.all_to_all(near_sum(chunks), FAR, 0, 0, tiled=True)
    grads = last(lax.all_gather(far_sum(chunks), "core", axis=0, tiled=False))

    pair = to_pair(pair).astype(F32)
    other = to_other(other).astype(F32)
    top = jnp.where(odd == 1, pair, other)
    bottom = jnp.where(odd == 1, other, pair)
    ends = jnp.stack([top, jnp.zeros_like(top), jnp.zeros_like(top), bottom])
    owned = slots.reshape(4, 16, D) + ends + sides[:4]
    node_sum = owned.reshape(64, D).astype(BF)
    mesh_grad = mm_nt(node_sum, w_em).reshape(4, 16, D)
    return (grid_grad.reshape(1, 1, 256, D), mesh_grad) + tuple(grads)


def solution(mesh):
    fine = Mesh(mesh.devices.reshape(tuple(SIZES.values())), tuple(SIZES))
    in_specs = (
        P(LAT, LON, None, None),
        P(LAT, LON, None),
        P(LAT, LON, None, None),
        P(LAT, LON, None, None),
        P(LAT, LON),
    ) + (P(),) * 7
    out_specs = (P(LAT, LON, None, None), P(LAT, LON, None)) + (P(LAT, None),) * 5
    return jax.shard_map(
        on_device, mesh=fine, in_specs=in_specs, out_specs=out_specs, check_vma=False
    )
```
